32 devices in a mesh: tm: 8 (over y, x, core), inp: 4 (over z).
Axes of the slice: x: 2, y: 2, z: 4, core: 2. Of those that a mesh axis runs over, the one named last changes fastest.
Arguments:
- voltages: bfloat16 [1024, 32768], P('inp', 'tm'), may hold values from -6 to 6
- input_gain: float32 [1024], P('inp'), may hold values from 0.5 to 2
- input_feed: int32 [1024], replicated, may hold values from 0 to 511
- beam_grid: int32 [1024], replicated, may hold values from 0 to 511
Outputs:
- visibilities: bfloat16 [512, 2, 1024, 1024], P(('tm', 'inp'))
- beam_power: float32 [512, 1024], P(('tm', 'inp'))
The draws below stay inside these ranges and needn't reach their ends.
All inputs are finite; a program needn't handle non-finite values.
Results may differ from the reference program's by a relative error of at most 0.0034.
Values may be sent and summed in bfloat16 or wider, within the bound.
No kernel may reach another device: no remote copies, remote signals or barrier semaphores. Data moves between devices by JAX's collectives and lax.ppermute only.
A program may use at most 128 MiB of HBM per device.

```python
import math
import jax
import jax.numpy as jnp
from jax import lax

INPUTS = 1024
L = 1024
CH = 512
BEAMS = 1024
TAPS = 4
GRID = 512
FRAMES = 32
SAMPLES = 32768


def draw_voltages(key, part):
    noise_key = jax.random.fold_in(key, 11)
    sky_key = jax.random.fold_in(key, 12)
    noise_part = jax.random.normal(noise_key, (INPUTS, SAMPLES), jnp.float32)
    common = jax.random.normal(sky_key, (1, SAMPLES), jnp.float32)
    return jnp.clip(0.6 * (noise_part + common), -6.0, 6.0).astype(jnp.bfloat16)


def place_ends(entries, key, smallest, top_value):
    place = [jax.random.randint(jax.random.fold_in(key, axis), (), 0, length) for axis, length in enumerate(entries.shape)]
    main_axis = entries.shape.index(max(entries.shape))
    neighbour = place[:main_axis] + [(place[main_axis] + 1) % entries.shape[main_axis]] + place[main_axis + 1:]
    return entries.at[tuple(place)].set(smallest).at[tuple(neighbour)].set(top_value)


def shard_levels(own_key, extent, shards, least, largest):
    def one(dim, parts):
        steps = jax.random.uniform(jax.random.fold_in(jax.random.fold_in(own_key, 6), dim), (parts,), jnp.float32, least / len(shards), largest / len(shards))
        return jnp.repeat(jnp.exp(steps), extent[dim] // parts).reshape((-1,) + (1,) * (len(extent) - dim - 1))

    gain = one(*shards[0])
    for cut in shards[1:]:
        gain = gain * one(*cut)
    return gain


def setup_inputs(seed: int = 0) -> dict:
    key_of = jax.random.split(jax.random.key(seed), 5)
    voltages = draw_voltages(jax.random.fold_in(key_of[4], 71), 0)
    input_gain = jnp.clip(jnp.exp(math.log(2.0) - 1.3862944 * jax.random.uniform(key_of[1], (INPUTS,), jnp.float32) ** shard_levels(key_of[1], (INPUTS,), ((0, 4),), -0.2, 0.2)), 0.5, 2.0)
    input_feed = place_ends(jax.random.randint(key_of[2], (INPUTS,), 0, GRID), jax.random.fold_in(key_of[2], 1), 0, GRID - 1).astype(jnp.int32)
    beam_grid = place_ends(jax.random.randint(key_of[3], (BEAMS,), 0, GRID), jax.random.fold_in(key_of[3], 1), 0, GRID - 1).astype(jnp.int32)
    return dict(voltages=voltages, input_gain=input_gain, input_feed=input_feed, beam_grid=beam_grid)


def window_table():
    span = TAPS * L
    sample_pos = jnp.arange(span).astype(jnp.float32)
    sinc_part = jnp.sinc((sample_pos - span / 2) / L)
    hann_part = 0.5 - 0.5 * jnp.cos(2.0 * jnp.pi * sample_pos / span)
    return (sinc_part * hann_part).reshape(TAPS, L)

def dft_table(channel):
    lag_index = jnp.arange(L).astype(jnp.int32)
    phase_step = lag_index[:, None] * channel[None, :] % L
    radians = 2.0 * jnp.pi * phase_step.astype(jnp.float32) / L
    factor = 1.0 / math.sqrt(L)
    stacked = jnp.stack([jnp.cos(radians), -jnp.sin(radians)], 2) * factor
    return stacked.astype(jnp.bfloat16).reshape(L, 2 * channel.shape[0])

def steer_table(input_feed, beam_grid):
    input_count = input_feed.shape[0]
    phase_step = input_feed[:, None] * beam_grid[None, :] % GRID
    radians = 2.0 * jnp.pi * phase_step.astype(jnp.float32) / GRID
    factor = 1.0 / math.sqrt(input_count)
    cosine = jnp.cos(radians) * factor
    sine_part = jnp.sin(radians) * factor
    top_rows = jnp.concatenate([cosine, sine_part], 1)
    low_rows = jnp.concatenate([-sine_part, cosine], 1)
    return jnp.concatenate([top_rows, low_rows], 0).astype(jnp.bfloat16)

def channel_products(spectrum, steer):
    real_part = spectrum[0]
    imag_part = spectrum[1]
    input_count = real_part.shape[0]
    frame_total = real_part.shape[1]
    stacked = jnp.concatenate([real_part, imag_part], 1)
    rotated = jnp.concatenate([imag_part, -real_part], 1)
    both = jnp.concatenate([stacked, rotated], 0)
    products = lax.dot_general(both, stacked, (((1,), (1,)), ((), ())), preferred_element_type=jnp.float32)
    visible = (products / frame_total).reshape(2, input_count, input_count).astype(jnp.bfloat16)
    flat = spectrum.reshape(2 * input_count, frame_total)
    beams = lax.dot_general(steer, flat, (((0,), (0,)), ((), ())), preferred_element_type=jnp.float32)
    beam_count = beams.shape[0] // 2
    power = lax.optimization_barrier(jnp.mean(beams[:beam_count] ** 2 + beams[beam_count:] ** 2, axis=1))
    return (visible, power)

def reference(voltages, input_gain, input_feed, beam_grid):
    per_block = 16
    window = window_table()
    table = dft_table(jnp.arange(CH).astype(jnp.int32))
    padded = jnp.concatenate([voltages, jnp.zeros((INPUTS, (TAPS - 1) * L), jnp.bfloat16)], 1)

    def one_block(items):
        block_rows, gains = items
        summed = jnp.zeros((per_block, FRAMES, L), jnp.float32)
        for tap in range(TAPS):
            piece = block_rows[:, tap * L:tap * L + FRAMES * L].reshape(per_block, FRAMES, L)
            summed = summed + piece.astype(jnp.float32) * window[tap]
        filtered = (summed * gains[:, None, None]).astype(jnp.bfloat16)
        spectra = jnp.dot(filtered.reshape(per_block * FRAMES, L), table, preferred_element_type=jnp.float32)
        return spectra.astype(jnp.bfloat16).reshape(per_block, FRAMES, CH, 2)
    spectra = lax.map(one_block, (padded.reshape(INPUTS // per_block, per_block, padded.shape[1]), input_gain.reshape(INPUTS // per_block, per_block)))
    spectra = spectra.reshape(INPUTS, FRAMES, CH, 2).transpose(2, 3, 0, 1)
    steer = steer_table(input_feed, beam_grid)
    visible, power = lax.map(lambda spectrum: channel_products(spectrum, steer), spectra)
    return (visible, power)
```

```python
import functools
import math

import jax
import jax.numpy as jnp
import numpy as np
from jax import lax
from jax.experimental import pallas as pl
from jax.experimental.pallas import tpu as pltpu
from jax.sharding import PartitionSpec as P

L = 1024
CH = 512
TAPS = 4
GRID = 512
SUB = 4
AXES = ("tm", "inp")
MIB = 2**20


def window_table():
    span = TAPS * L
    pos = np.arange(span, dtype=np.float64)
    window = np.sinc((pos - span / 2) / L) * (0.5 - 0.5 * np.cos(2.0 * np.pi * pos / span))
    return window.astype(np.float32).reshape(TAPS, L)


def dft_rows():
    step = np.arange(CH)[:, None] * np.arange(L)[None, :] % L
    radians = 2.0 * np.pi * step / L
    both = np.stack([np.cos(radians), -np.sin(radians)], 1) / math.sqrt(L)
    return both.reshape(2 * CH, L).astype(jnp.bfloat16)


def steer_grid(input_count):
    step = np.arange(GRID)[:, None] * np.arange(GRID)[None, :] % GRID
    radians = 2.0 * np.pi * step / GRID
    both = np.stack([np.cos(radians), np.sin(radians)], 0) / math.sqrt(input_count)
    return both.astype(jnp.bfloat16)


def sort_rows(slots):
    order = np.arange(slots * SUB * 2).reshape(slots, SUB, 2).transpose(1, 2, 0).reshape(-1)
    return np.eye(slots * SUB * 2, dtype=np.float32)[order].astype(jnp.bfloat16)


def channelize_kernel(frames, cuts, v_ref, later_ref, gain_ref, window_ref, table_ref, *out_refs):
    frame_count = v_ref.shape[1] // L
    dests = out_refs[0].shape[0]
    for at, frame in enumerate(frames):
        total = None
        for tap in range(TAPS):
            source = frame + tap
            if source < frame_count:
                piece = v_ref[:, source * L : (source + 1) * L]
            else:
                piece = later_ref[:, (source - frame_count) * L : (source - frame_count + 1) * L]
            term = piece.astype(jnp.float32) * window_ref[tap : tap + 1, :]
            total = term if total is None else total + term
        filtered = (total * gain_ref[...]).astype(jnp.bfloat16)
        spectra = lax.dot_general(
            table_ref[...], filtered, (((1,), (1,)), ((), ())), preferred_element_type=jnp.float32
        ).astype(jnp.bfloat16)
        spectra = spectra.reshape(dests, spectra.shape[0] // dests, spectra.shape[1])
        row = 0
        for out_ref, rows in zip(out_refs, cuts):
            out_ref[:, at * rows : (at + 1) * rows, :] = spectra[:, row : row + rows, :]
            row += rows


def channelize(frames, cuts, dests, voltages, later, gain, window, table):
    rows = voltages.shape[0]
    cost = pl.CostEstimate(
        flops=2 * len(frames) * rows * L * 2 * CH,
        bytes_accessed=2 * (voltages.size + table.size + len(frames) * rows * 2 * CH),
        transcendentals=0,
    )
    return pl.pallas_call(
        functools.partial(channelize_kernel, frames, cuts),
        out_shape=[
            jax.ShapeDtypeStruct((dests, len(frames) * cut, rows), jnp.bfloat16) for cut in cuts
        ],
        compiler_params=pltpu.CompilerParams(vmem_limit_bytes=32 * MIB),
        cost_estimate=cost,
        name="channelize",
    )(voltages, later, gain, window, table)


def steer_kernel(feed_ref, beam_ref, table_ref, out_ref):
    inputs = feed_ref.shape[0]
    beams = beam_ref.shape[1]
    feed = lax.rem(feed_ref[...], GRID)
    beam = lax.rem(beam_ref[...], GRID)
    pick_feed = (lax.broadcasted_iota(jnp.int32, (inputs, GRID), 1) == feed)
    pick_feed = pick_feed.astype(jnp.float32).astype(jnp.bfloat16)
    pick_beam = (lax.broadcasted_iota(jnp.int32, (GRID, beams), 0) == beam)
    pick_beam = pick_beam.astype(jnp.float32).astype(jnp.bfloat16)
    for part in range(2):
        rows = jnp.dot(pick_feed, table_ref[part], preferred_element_type=jnp.float32)
        out_ref[part] = jnp.dot(
            rows.astype(jnp.bfloat16), pick_beam, preferred_element_type=jnp.float32
        ).astype(jnp.bfloat16)


def steering(input_feed, beam_grid, table):
    inputs, beams = input_feed.shape[0], beam_grid.shape[0]
    cost = pl.CostEstimate(
        flops=4 * inputs * GRID * (GRID + beams), bytes_accessed=4 * inputs * beams, transcendentals=0
    )
    return pl.pallas_call(
        steer_kernel,
        out_shape=jax.ShapeDtypeStruct((2, inputs, beams), jnp.bfloat16),
        compiler_params=pltpu.CompilerParams(vmem_limit_bytes=32 * MIB),
        cost_estimate=cost,
        name="steering",
    )(input_feed.reshape(inputs, 1), beam_grid.reshape(1, beams), table)


def products_kernel(
    n_time, n_input, frame_count, first, count, x0_ref, xl_ref, sort_ref, steer_ref, *rest
):
    vis_ref, power_ref, arrived, ordered = rest[-4:]
    step = pl.program_id(0)
    half = n_time * frame_count
    rows_per = 2 * half
    width = x0_ref.shape[2]
    inputs = n_input * width
    tile = 2 * SUB

    @pl.when(step % SUB == 0)
    def _():
        sub = step // SUB
        for t in range(n_time):
            for i in range(n_input):
                source = t * n_input + i
                lanes = slice(i * width, (i + 1) * width)
                for f in range(frame_count):
                    slot = (t * frame_count + f) * tile
                    if f == 0:
                        at = pl.multiple_of((first // SUB + sub) * tile, tile)
                        piece = x0_ref[source, pl.ds(at, tile), :]
                    else:
                        at = pl.multiple_of(((f - 1) * (count // SUB) + sub) * tile, tile)
                        piece = xl_ref[source, pl.ds(at, tile), :]
                    arrived[slot : slot + tile, lanes] = piece
        sorted_rows = jnp.dot(sort_ref[...], arrived[...], preferred_element_type=jnp.float32)
        ordered[...] = sorted_rows.astype(jnp.bfloat16)
        beams = steer_ref.shape[2]
        chunk = min(beams, 256)
        for b in range(0, beams, chunk):
            lanes = slice(b, b + chunk)
            cos_part = jnp.dot(ordered[...], steer_ref[0, :, lanes], preferred_element_type=jnp.float32)
            sin_part = jnp.dot(ordered[...], steer_ref[1, :, lanes], preferred_element_type=jnp.float32)
            for c in range(SUB):
                re = slice(c * rows_per, c * rows_per + half)
                im = slice(c * rows_per + half, (c + 1) * rows_per)
                beam_re = cos_part[re] - sin_part[im]
                beam_im = sin_part[re] + cos_part[im]
                power = jnp.sum(beam_re * beam_re + beam_im * beam_im, axis=0, keepdims=True)
                power_ref[0, c : c + 1, lanes] = power * (1.0 / half)

    at = pl.multiple_of((step % SUB) * rows_per, rows_per)
    both = ordered[pl.ds(at, rows_per), :]
    re, im = both[:half], both[half:]
    left = jnp.concatenate([re, im, im, -re], 0).T
    right = both * jnp.asarray(1.0 / half, jnp.bfloat16)
    zero = jnp.zeros_like(right)
    chunk = min(inputs, 256)
    for part in range(2):
        against = jnp.concatenate([right, zero] if part == 0 else [zero, right], 0)
        for b in range(0, inputs, chunk):
            lanes = slice(b, b + chunk)
            vis_ref[0, part, :, lanes] = jnp.dot(
                left, against[:, lanes], preferred_element_type=jnp.float32
            ).astype(jnp.bfloat16)


def products(sizes, first, count, x0, xl, sort, steer, so_far):
    n_time, n_input, frame_count, per_dev = sizes
    inputs = n_input * x0.shape[2]
    beams = steer.shape[2]
    whole = pl.BlockSpec(memory_space=pltpu.VMEM)
    rows = 2 * n_time * frame_count * SUB
    cost = pl.CostEstimate(
        flops=count * 2 * rows // SUB * inputs * (2 * inputs + 2 * beams),
        bytes_accessed=count * 4 * inputs * inputs + 4 * inputs * beams,
        transcendentals=0,
    )
    operands = [x0, xl, sort, steer]
    specs = [whole] * 4
    aliases = {}
    if so_far is not None:
        aliases = {len(operands): 0}
        operands.append(so_far)
        specs.append(pl.BlockSpec(memory_space=pl.ANY))
    vis, power = pl.pallas_call(
        functools.partial(products_kernel, n_time, n_input, frame_count, first, count),
        grid=(count,),
        in_specs=specs,
        out_specs=[
            pl.BlockSpec((1, 2, inputs, inputs), lambda c: (first + c, 0, 0, 0)),
            pl.BlockSpec((1, SUB, beams), lambda c: (c // SUB, 0, 0)),
        ],
        out_shape=[
            jax.ShapeDtypeStruct((per_dev, 2, inputs, inputs), jnp.bfloat16),
            jax.ShapeDtypeStruct((count // SUB, SUB, beams), jnp.float32),
        ],
        scratch_shapes=[
            pltpu.VMEM((rows, inputs), jnp.bfloat16),
            pltpu.VMEM((rows, inputs), jnp.bfloat16),
        ],
        input_output_aliases=aliases,
        compiler_params=pltpu.CompilerParams(vmem_limit_bytes=40 * MIB),
        cost_estimate=cost,
        name="products",
    )(*operands)
    return vis, power.reshape(count, beams)


def exchanged(block):
    return lax.all_to_all(block, AXES, 0, 0, tiled=True)


def in_pieces(voltages, input_gain, input_feed, beam_grid):
    frame_count = voltages.shape[1] // L
    n_time = lax.axis_size("tm")
    n_input = lax.axis_size("inp")
    dests = n_time * n_input
    per_dev = CH // dests
    last = max(SUB, per_dev // 4 // SUB * SUB)
    counts = (per_dev - last, last)

    later = lax.ppermute(
        voltages[:, : (TAPS - 1) * L], "tm", [(i + 1, i) for i in range(n_time - 1)]
    )
    window = jnp.asarray(window_table())
    table = jnp.asarray(dft_rows())
    gain = input_gain.reshape(-1, 1)
    sort = jnp.asarray(sort_rows(n_time * frame_count))

    (first_frame,) = channelize(
        (0,), (2 * per_dev,), dests, voltages, voltages[:8, :128], gain, window, table
    )
    x0 = exchanged(first_frame)
    parts = channelize(
        tuple(range(1, frame_count)),
        tuple(2 * c for c in counts),
        dests,
        voltages,
        later,
        gain,
        window,
        table,
    )
    steer = steering(input_feed, beam_grid, jnp.asarray(steer_grid(input_feed.shape[0])))
    send_a, x0, steer = lax.optimization_barrier((parts[0], x0, steer))
    xa = exchanged(send_a)
    send_b, xa = lax.optimization_barrier((parts[1], xa))
    xb = exchanged(send_b)
    sizes = (n_time, n_input, frame_count, per_dev)
    vis, power_a = products(sizes, 0, counts[0], x0, xa, sort, steer, None)
    vis, power_b = products(sizes, counts[0], counts[1], x0, xb, sort, steer, vis)
    return vis, jnp.concatenate([power_a, power_b], 0)


def whole_channel(spectrum, steer):
    real_part, imag_part = spectrum[0], spectrum[1]
    input_count, frame_total = real_part.shape
    stacked = jnp.concatenate([real_part, imag_part], 1)
    rotated = jnp.concatenate([imag_part, -real_part], 1)
    both = jnp.concatenate([stacked, rotated], 0)
    found = lax.dot_general(
        both, stacked, (((1,), (1,)), ((), ())), preferred_element_type=jnp.float32
    )
    visible = (found / frame_total).reshape(2, input_count, input_count).astype(jnp.bfloat16)
    cos_part, sin_part = [
        lax.dot_general(
            spectrum, part, (((1,), (0,)), ((), ())), preferred_element_type=jnp.float32
        )
        for part in steer
    ]
    beam_re = cos_part[0] - sin_part[1]
    beam_im = sin_part[0] + cos_part[1]
    return visible, jnp.mean(beam_re**2 + beam_im**2, axis=0)


def at_once(voltages, input_gain, input_feed, beam_grid):
    rows = voltages.shape[0]
    frame_count = voltages.shape[1] // L
    n_time = lax.axis_size("tm")
    n_input = lax.axis_size("inp")
    dests = n_time * n_input
    per_dev = CH // dests
    later = lax.ppermute(
        voltages[:, : (TAPS - 1) * L], "tm", [(i + 1, i) for i in range(n_time - 1)]
    )
    joined = jnp.concatenate([voltages, later], 1)
    window = jnp.asarray(window_table())
    summed = jnp.zeros((rows, frame_count, L), jnp.float32)
    for tap in range(TAPS):
        piece = joined[:, tap * L : (tap + frame_count) * L].reshape(rows, frame_count, L)
        summed = summed + piece.astype(jnp.float32) * window[tap]
    filtered = (summed * input_gain[:, None, None]).astype(jnp.bfloat16)
    spectra = lax.dot_general(
        jnp.asarray(dft_rows()),
        filtered,
        (((1,), (2,)), ((), ())),
        preferred_element_type=jnp.float32,
    ).astype(jnp.bfloat16)
    blocks = exchanged(spectra.reshape(dests, per_dev * 2, rows, frame_count))
    blocks = blocks.reshape(n_time, n_input, per_dev, 2, rows, frame_count)
    owned = blocks.transpose(2, 3, 1, 4, 0, 5)
    owned = owned.reshape(per_dev, 2, n_input * rows, n_time * frame_count)
    steer = steering(input_feed, beam_grid, jnp.asarray(steer_grid(input_feed.shape[0])))
    return lax.map(lambda spectrum: whole_channel(spectrum, steer), owned)


def on_device(voltages, input_gain, input_feed, beam_grid):
    per_dev = CH // (lax.axis_size("tm") * lax.axis_size("inp"))
    slots = lax.axis_size("tm") * (voltages.shape[1] // L)
    if per_dev % SUB == 0 and per_dev >= 2 * SUB and slots % 16 == 0 and slots & (slots - 1) == 0:
        return in_pieces(voltages, input_gain, input_feed, beam_grid)
    return at_once(voltages, input_gain, input_feed, beam_grid)


def solution(mesh):
    return jax.shard_map(
        on_device,
        mesh=mesh,
        in_specs=(P("inp", "tm"), P("inp"), P(), P()),
        out_specs=(P(("tm", "inp"), None, None, None), P(("tm", "inp"), None)),
        check_vma=False,
    )
```

```python
import functools
import math

import jax
import jax.numpy as jnp
import numpy as np
from jax import lax
from jax.experimental import pallas as pl
from jax.experimental.pallas import tpu as pltpu
from jax.sharding import PartitionSpec as P

L = 1024
CH = 512
TAPS = 4
GRID = 512
SUB = 4
AXES = ("tm", "inp")
MIB = 2**20


def window_table():
    span = TAPS * L
    pos = np.arange(span, dtype=np.float64)
    window = np.sinc((pos - span / 2) / L) * (0.5 - 0.5 * np.cos(2.0 * np.pi * pos / span))
    return window.astype(np.float32).reshape(TAPS, L)


def dft_rows():
    step = np.arange(CH)[:, None] * np.arange(L)[None, :] % L
    radians = 2.0 * np.pi * step / L
    both = np.stack([np.cos(radians), -np.sin(radians)], 1) / math.sqrt(L)
    return both.reshape(2 * CH, L).astype(jnp.bfloat16)


def steer_grid(input_count):
    step = np.arange(GRID)[:, None] * np.arange(GRID)[None, :] % GRID
    radians = 2.0 * np.pi * step / GRID
    both = np.stack([np.cos(radians), np.sin(radians)], 0) / math.sqrt(input_count)
    return both.astype(jnp.bfloat16)


def filtered_frame(pieces, gain_ref, window_ref):
    total = None
    for tap, piece in enumerate(pieces):
        term = piece.astype(jnp.float32) * window_ref[tap : tap + 1, :]
        total = term if total is None else total + term
    rows = total.shape[0]
    gain = jnp.broadcast_to(gain_ref[...], (128, rows)).T[:, :1]
    return (total * gain).astype(jnp.bfloat16)


def put_spectra(filtered, table_ref, outs):
    spectra = lax.dot_general(
        table_ref[...], filtered, (((1,), (1,)), ((), ())), preferred_element_type=jnp.float32
    ).astype(jnp.bfloat16)
    dests = outs[0].shape[0]
    spectra = spectra.reshape(dests, spectra.shape[0] // dests, spectra.shape[1])
    row = 0
    for out in outs:
        rows = out.shape[-2]
        if len(out.shape) == 4:
            out[:, 0] = spectra[:, row : row + rows]
        else:
            out[...] = spectra[:, row : row + rows]
        row += rows


def frame_of(ref, frame):
    return ref[:, frame * L : (frame + 1) * L]


def heads_kernel(v_ref, *refs):
    head_refs, held, sems = refs[:-2], refs[-2], refs[-1]
    into, out, start = [], [], 0
    for at, head_ref in enumerate(head_refs):
        lanes = slice(start, start + head_ref.shape[1])
        into.append(pltpu.make_async_copy(v_ref.at[:, lanes], held.at[:, lanes], sems.at[0, at]))
        out.append(pltpu.make_async_copy(held.at[:, lanes], head_ref, sems.at[1, at]))
        into[-1].start()
        start = lanes.stop
    for first, second in zip(into, out):
        first.wait()
        second.start()
    for copy in out:
        copy.wait()


def heads_of(voltages, widths):
    rows, span = voltages.shape[0], sum(widths)
    far = pl.BlockSpec(memory_space=pltpu.HBM)
    return pl.pallas_call(
        heads_kernel,
        in_specs=[far],
        out_specs=[far] * len(widths),
        out_shape=[jax.ShapeDtypeStruct((rows, width), jnp.bfloat16) for width in widths],
        scratch_shapes=[
            pltpu.VMEM((rows, span), jnp.bfloat16),
            pltpu.SemaphoreType.DMA((2, len(widths))),
        ],
        compiler_params=pltpu.CompilerParams(vmem_limit_bytes=58 * MIB),
        cost_estimate=pl.CostEstimate(flops=0, bytes_accessed=4 * rows * span, transcendentals=0),
        name="heads",
    )(voltages)


def first_kernel(v_ref, gain_ref, window_ref, table_ref, out_ref, held, gain, window, table, sems):
    copies = [
        pltpu.make_async_copy(frame_of(v_ref.at, tap), frame_of(held.at, tap), sems.at[tap])
        for tap in range(TAPS)
    ]
    copies.append(pltpu.make_async_copy(window_ref, window, sems.at[TAPS]))
    copies.append(pltpu.make_async_copy(gain_ref, gain, sems.at[TAPS + 1]))
    for copy in copies:
        copy.start()
    table_copy = pltpu.make_async_copy(table_ref, table, sems.at[TAPS + 2])
    table_copy.start()
    for copy in copies:
        copy.wait()
    filtered = filtered_frame([frame_of(held, tap) for tap in range(TAPS)], gain, window)
    table_copy.wait()
    put_spectra(filtered, table, [out_ref])


def first_frame(dests, voltages, gain, window, table):
    rows = voltages.shape[0]
    far = pl.BlockSpec(memory_space=pltpu.HBM)
    return pl.pallas_call(
        first_kernel,
        in_specs=[far] * 4,
        out_shape=jax.ShapeDtypeStruct((dests, 2 * CH // dests, rows), jnp.bfloat16),
        scratch_shapes=[
            pltpu.VMEM((rows, TAPS * L), jnp.bfloat16),
            pltpu.VMEM(gain.shape, jnp.float32),
            pltpu.VMEM(window.shape, jnp.float32),
            pltpu.VMEM(table.shape, jnp.bfloat16),
            pltpu.SemaphoreType.DMA((TAPS + 3,)),
        ],
        compiler_params=pltpu.CompilerParams(vmem_limit_bytes=58 * MIB),
        cost_estimate=pl.CostEstimate(
            flops=2 * rows * L * 2 * CH, bytes_accessed=4 * voltages.size, transcendentals=0
        ),
        name="first_frame",
    )(voltages, gain, window, table)


def later_kernel(frame, n_later, n_out, v_ref, gain_ref, window_ref, table_ref, *refs):
    frame_count = v_ref.shape[1] // L
    later_refs, out_refs = refs[:n_later], refs[-n_out:]
    frames = [frame_of(v_ref, source) for source in range(frame_count)]
    for ref in later_refs:
        frames += [frame_of(ref, source) for source in range(ref.shape[1] // L)]
    pieces = frames[frame : frame + TAPS]
    put_spectra(filtered_frame(pieces, gain_ref, window_ref), table_ref, out_refs)


def later_frame(frame, dests, cuts, voltages, later, gain, window, table, so_far):
    rows = voltages.shape[0]
    frame_count = voltages.shape[1] // L
    needed = frame + TAPS - frame_count
    later = [block for at, block in enumerate(later) if sum(b.shape[1] for b in later[:at]) < needed * L]
    whole = pl.BlockSpec(memory_space=pltpu.VMEM)
    operands = [voltages, gain, window, table, *later]
    specs = [whole] * len(operands)
    aliases = {}
    for at, block in enumerate(so_far):
        aliases[len(operands)] = at
        operands.append(block)
        specs.append(pl.BlockSpec(memory_space=pl.ANY))
    return pl.pallas_call(
        functools.partial(later_kernel, frame, len(later), len(cuts)),
        grid=(1,),
        in_specs=specs,
        out_specs=[
            pl.BlockSpec((dests, 1, cut, rows), lambda g: (0, frame - 1, 0, 0)) for cut in cuts
        ],
        out_shape=[
            jax.ShapeDtypeStruct((dests, frame_count - 1, cut, rows), jnp.bfloat16) for cut in cuts
        ],
        input_output_aliases=aliases,
        compiler_params=pltpu.CompilerParams(vmem_limit_bytes=24 * MIB),
        cost_estimate=pl.CostEstimate(
            flops=2 * rows * L * 2 * CH, bytes_accessed=3 * voltages.size, transcendentals=0
        ),
        name="later_frame",
    )(*operands)


def steer_kernel(feed_ref, beam_ref, table_ref, out_ref):
    inputs = feed_ref.shape[0]
    chunks, width = out_ref.shape[0], out_ref.shape[2] // 2
    beams = chunks * width
    feed = lax.rem(feed_ref[...], GRID)
    beam = lax.rem(beam_ref[...], GRID)
    pick_feed = (lax.broadcasted_iota(jnp.int32, (inputs, GRID), 1) == feed)
    pick_feed = pick_feed.astype(jnp.float32).astype(jnp.bfloat16)
    pick_beam = (lax.broadcasted_iota(jnp.int32, (GRID, beams), 0) == beam)
    pick_beam = pick_beam.astype(jnp.float32).astype(jnp.bfloat16)
    for part in range(2):
        rows = jnp.dot(pick_feed, table_ref[part], preferred_element_type=jnp.float32)
        found = jnp.dot(rows.astype(jnp.bfloat16), pick_beam, preferred_element_type=jnp.float32)
        for c in range(chunks):
            out_ref[c, :, part * width : (part + 1) * width] = found[
                :, c * width : (c + 1) * width
            ].astype(jnp.bfloat16)


def steering(input_feed, beam_grid, table, chunks):
    inputs, beams = input_feed.shape[0], beam_grid.shape[0]
    cost = pl.CostEstimate(
        flops=4 * inputs * GRID * (GRID + beams), bytes_accessed=4 * inputs * beams, transcendentals=0
    )
    return pl.pallas_call(
        steer_kernel,
        out_shape=jax.ShapeDtypeStruct((chunks, inputs, 2 * beams // chunks), jnp.bfloat16),
        compiler_params=pltpu.CompilerParams(vmem_limit_bytes=32 * MIB),
        cost_estimate=cost,
        name="steering",
    )(input_feed.reshape(inputs, 1), beam_grid.reshape(1, beams), table)


def products_kernel(
    n_time, n_input, frame_count, first, count, x0_ref, xl_ref, steer_ref, *rest
):
    vis_ref, power_ref, arrived, ordered, held, ring, sems, ring_sems = rest[-8:]
    step, steps = pl.program_id(0), pl.num_programs(0)
    chunk = step % SUB
    slots = ring.shape[0]

    def vis_copy(at, part):
        slot = at % slots
        return pltpu.make_async_copy(
            ring.at[slot, part], vis_ref.at[first + at, part], ring_sems.at[slot, part]
        )

    def steer_copy(c):
        return pltpu.make_async_copy(steer_ref.at[c], held.at[c], sems.at[c])

    @pl.when(step == 0)
    def _():
        steer_copy(0).start()

    half = n_time * frame_count
    rows_per = 2 * half
    width = x0_ref.shape[2]
    inputs = n_input * width
    tile = 2 * SUB

    @pl.when(step % SUB == 0)
    def _():
        sub = step // SUB
        at = pl.multiple_of((first // SUB + sub) * tile, tile)
        at_later = pl.multiple_of(sub * tile, tile)
        for t in range(n_time):
            for i in range(n_input):
                source = t * n_input + i
                lanes = slice(i * width, (i + 1) * width)
                for f in range(frame_count):
                    slot = (t * frame_count + f) * tile
                    if f == 0:
                        piece = x0_ref[source, pl.ds(at, tile), :]
                    else:
                        piece = xl_ref[source, f - 1, pl.ds(at_later, tile), :]
                    arrived[slot : slot + tile, lanes] = piece
        total = SUB * rows_per
        row = lax.broadcasted_iota(jnp.int32, (total, total), 0)
        column = lax.broadcasted_iota(jnp.int32, (total, total), 1)
        source = (row % half) * tile + (row // rows_per) * 2 + (row // half) % 2
        pick = jnp.where(column == source, 1.0, 0.0).astype(jnp.bfloat16)
        sorted_rows = jnp.dot(pick, arrived[...], preferred_element_type=jnp.float32)
        ordered[...] = sorted_rows.astype(jnp.bfloat16)

    @pl.when(step < SUB)
    def _():
        steer_copy(chunk).wait()

    @pl.when(step == 0)
    def _():
        for c in range(1, SUB):
            steer_copy(c).start()

    @pl.when(step >= slots)
    def _():
        for part in range(2):
            vis_copy(step - slots, part).wait()

    at = pl.multiple_of((step % SUB) * rows_per, rows_per)
    both = ordered[pl.ds(at, rows_per), :]
    re, im = both[:half], both[half:]
    right = both * jnp.asarray(1.0 / half, jnp.bfloat16)
    wide = steer_ref.shape[2] // 2
    turned = jnp.dot(ordered[...], held[chunk], preferred_element_type=jnp.float32)
    cos_part, sin_part = turned[:, :wide], turned[:, wide:]
    lanes = pl.ds(pl.multiple_of(chunk * wide, wide), wide)
    for c in range(SUB):
        rows_re = slice(c * rows_per, c * rows_per + half)
        rows_im = slice(c * rows_per + half, (c + 1) * rows_per)
        beam_re = cos_part[rows_re] - sin_part[rows_im]
        beam_im = sin_part[rows_re] + cos_part[rows_im]
        power = jnp.sum(beam_re * beam_re + beam_im * beam_im, axis=0, keepdims=True)
        row = (step // SUB) % 2 * SUB + c
        power_ref[pl.ds(row, 1), lanes] = power * (1.0 / half)

    block = min(inputs, 256)
    slot = step % slots
    for part in range(2):
        left = (both if part == 0 else jnp.concatenate([im, -re], 0)).T
        for j in range(0, inputs, block):
            lanes = slice(j, j + block)
            upper = jnp.dot(
                left[: j + block], right[:, lanes], preferred_element_type=jnp.float32
            ).astype(jnp.bfloat16)
            ring[slot, part, : j + block, lanes] = upper
            for i in range(0, j, block):
                mirror = upper[i : i + block].T
                ring[slot, part, lanes, i : i + block] = mirror if part == 0 else -mirror
        vis_copy(step, part).start()

    @pl.when(step == steps - 1)
    def _():
        for at in range(count - min(slots, count), count):
            for part in range(2):
                vis_copy(at, part).wait()


def products(sizes, first, count, x0, xl, steer, so_far):
    n_time, n_input, frame_count, per_dev = sizes
    inputs = n_input * x0.shape[2]
    beams = steer.shape[0] * steer.shape[2] // 2
    whole = pl.BlockSpec(memory_space=pltpu.VMEM)
    rows = 2 * n_time * frame_count * SUB
    slots = min(3, count)
    cost = pl.CostEstimate(
        flops=count * 2 * rows // SUB * inputs * (2 * inputs + 2 * beams),
        bytes_accessed=count * 4 * inputs * inputs + 4 * inputs * beams,
        transcendentals=0,
    )
    operands = [x0, xl, steer]
    specs = [whole] * 2 + [pl.BlockSpec(memory_space=pltpu.HBM)]
    aliases = {}
    for at, block in enumerate(so_far):
        aliases[len(operands)] = at
        operands.append(block)
        specs.append(pl.BlockSpec(memory_space=pl.ANY))
    return pl.pallas_call(
        functools.partial(products_kernel, n_time, n_input, frame_count, first, count),
        grid=(count,),
        in_specs=specs,
        out_specs=[
            pl.BlockSpec(memory_space=pltpu.HBM),
            pl.BlockSpec((2 * SUB, beams), lambda c: ((first + c) // (2 * SUB), 0)),
        ],
        out_shape=[
            jax.ShapeDtypeStruct((per_dev, 2, inputs, inputs), jnp.bfloat16),
            jax.ShapeDtypeStruct((per_dev, beams), jnp.float32),
        ],
        scratch_shapes=[
            pltpu.VMEM((rows, inputs), jnp.bfloat16),
            pltpu.VMEM((rows, inputs), jnp.bfloat16),
            pltpu.VMEM(steer.shape, jnp.bfloat16),
            pltpu.VMEM((slots, 2, inputs, inputs), jnp.bfloat16),
            pltpu.SemaphoreType.DMA((SUB,)),
            pltpu.SemaphoreType.DMA((slots, 2)),
        ],
        input_output_aliases=aliases,
        compiler_params=pltpu.CompilerParams(vmem_limit_bytes=58 * MIB),
        cost_estimate=cost,
        name="products",
    )(*operands)


def exchanged(block):
    return lax.all_to_all(block, AXES, 0, 0, tiled=True)


def in_pieces(voltages, input_gain, input_feed, beam_grid):
    frame_count = voltages.shape[1] // L
    n_time = lax.axis_size("tm")
    n_input = lax.axis_size("inp")
    dests = n_time * n_input
    per_dev = CH // dests
    last = per_dev // 2 // (2 * SUB) * (2 * SUB)
    counts = (per_dev - last, last)
    back = [(i + 1, i) for i in range(n_time - 1)]

    window = jnp.asarray(window_table())
    table = jnp.asarray(dft_rows())
    gain = input_gain.reshape(1, -1)

    widths = ((TAPS - 2) * L, L)
    later = [lax.ppermute(head, "tm", back) for head in heads_of(voltages, widths)]
    first = first_frame(dests, voltages, gain, window, table)
    x0 = exchanged(first)
    parts = ()
    for frame in range(1, frame_count):
        cuts = [2 * count for count in counts]
        parts = later_frame(frame, dests, cuts, voltages, later, gain, window, table, parts)
    steer = steering(input_feed, beam_grid, jnp.asarray(steer_grid(input_feed.shape[0])), SUB)
    send_a, x0, steer = lax.optimization_barrier((parts[0], x0, steer))
    xa = exchanged(send_a)
    send_b, xa = lax.optimization_barrier((parts[1], xa))
    xb = exchanged(send_b)
    sizes = (n_time, n_input, frame_count, per_dev)
    found = products(sizes, 0, counts[0], x0, xa, steer, ())
    return products(sizes, counts[0], counts[1], x0, xb, steer, found)


def whole_channel(spectrum, steer):
    real_part, imag_part = spectrum[0], spectrum[1]
    input_count, frame_total = real_part.shape
    stacked = jnp.concatenate([real_part, imag_part], 1)
    rotated = jnp.concatenate([imag_part, -real_part], 1)
    both = jnp.concatenate([stacked, rotated], 0)
    found = lax.dot_general(
        both, stacked, (((1,), (1,)), ((), ())), preferred_element_type=jnp.float32
    )
    visible = (found / frame_total).reshape(2, input_count, input_count).astype(jnp.bfloat16)
    cos_part, sin_part = [
        lax.dot_general(
            spectrum, part, (((1,), (0,)), ((), ())), preferred_element_type=jnp.float32
        )
        for part in steer
    ]
    beam_re = cos_part[0] - sin_part[1]
    beam_im = sin_part[0] + cos_part[1]
    return visible, jnp.mean(beam_re**2 + beam_im**2, axis=0)


def at_once(voltages, input_gain, input_feed, beam_grid):
    rows = voltages.shape[0]
    frame_count = voltages.shape[1] // L
    n_time = lax.axis_size("tm")
    n_input = lax.axis_size("inp")
    dests = n_time * n_input
    per_dev = CH // dests
    later = lax.ppermute(
        voltages[:, : (TAPS - 1) * L], "tm", [(i + 1, i) for i in range(n_time - 1)]
    )
    joined = jnp.concatenate([voltages, later], 1)
    window = jnp.asarray(window_table())
    summed = jnp.zeros((rows, frame_count, L), jnp.float32)
    for tap in range(TAPS):
        piece = joined[:, tap * L : (tap + frame_count) * L].reshape(rows, frame_count, L)
        summed = summed + piece.astype(jnp.float32) * window[tap]
    filtered = (summed * input_gain[:, None, None]).astype(jnp.bfloat16)
    spectra = lax.dot_general(
        jnp.asarray(dft_rows()),
        filtered,
        (((1,), (2,)), ((), ())),
        preferred_element_type=jnp.float32,
    ).astype(jnp.bfloat16)
    blocks = exchanged(spectra.reshape(dests, per_dev * 2, rows, frame_count))
    blocks = blocks.reshape(n_time, n_input, per_dev, 2, rows, frame_count)
    owned = blocks.transpose(2, 3, 1, 4, 0, 5)
    owned = owned.reshape(per_dev, 2, n_input * rows, n_time * frame_count)
    steer = steering(input_feed, beam_grid, jnp.asarray(steer_grid(input_feed.shape[0])), 1)[0]
    steer = jnp.split(steer, 2, axis=1)
    return lax.map(lambda spectrum: whole_channel(spectrum, steer), owned)


def on_device(voltages, input_gain, input_feed, beam_grid):
    per_dev = CH // (lax.axis_size("tm") * lax.axis_size("inp"))
    slots = lax.axis_size("tm") * (voltages.shape[1] // L)
    whole_tiles = per_dev % (4 * SUB) == 0 and slots % 16 == 0 and beam_grid.shape[0] % (SUB * 128) == 0
    if whole_tiles and slots & (slots - 1) == 0:
        return in_pieces(voltages, input_gain, input_feed, beam_grid)
    return at_once(voltages, input_gain, input_feed, beam_grid)


def solution(mesh):
    return jax.shard_map(
        on_device,
        mesh=mesh,
        in_specs=(P("inp", "tm"), P("inp"), P(), P()),
        out_specs=(P(("tm", "inp"), None, None, None), P(("tm", "inp"), None)),
        check_vma=False,
    )
```

```python
import functools
import math

import jax
import jax.numpy as jnp
import numpy as np
from jax import lax
from jax.experimental import pallas as pl
from jax.experimental.pallas import tpu as pltpu
from jax.sharding import PartitionSpec as P

L = 1024
CH = 512
TAPS = 4
GRID = 512
SUB = 4
LAST_GROUP = 2 * SUB
AXES = ("tm", "inp")
MIB = 2**20


def window_table():
    span = TAPS * L
    pos = np.arange(span, dtype=np.float64)
    window = np.sinc((pos - span / 2) / L) * (0.5 - 0.5 * np.cos(2.0 * np.pi * pos / span))
    return window.astype(np.float32).reshape(TAPS, L)


def dft_rows():
    step = np.arange(CH)[:, None] * np.arange(L)[None, :] % L
    radians = 2.0 * np.pi * step / L
    both = np.stack([np.cos(radians), -np.sin(radians)], 1) / math.sqrt(L)
    return both.reshape(2 * CH, L).astype(jnp.bfloat16)


def steer_grid(input_count):
    step = np.arange(GRID)[:, None] * np.arange(GRID)[None, :] % GRID
    radians = 2.0 * np.pi * step / GRID
    both = np.stack([np.cos(radians), np.sin(radians)], 0) / math.sqrt(input_count)
    return both.astype(jnp.bfloat16)


def filtered_frame(pieces, gain_ref, window_ref):
    total = None
    for tap, piece in enumerate(pieces):
        term = piece.astype(jnp.float32) * window_ref[tap : tap + 1, :]
        total = term if total is None else total + term
    rows = total.shape[0]
    gain = jnp.broadcast_to(gain_ref[...], (128, rows)).T[:, :1]
    return (total * gain).astype(jnp.bfloat16)


def put_spectra(filtered, table_ref, outs):
    spectra = lax.dot_general(
        table_ref[...], filtered, (((1,), (1,)), ((), ())), preferred_element_type=jnp.float32
    ).astype(jnp.bfloat16)
    dests = outs[0].shape[0]
    spectra = spectra.reshape(dests, spectra.shape[0] // dests, spectra.shape[1])
    row = 0
    for out in outs:
        rows = out.shape[-2]
        if len(out.shape) == 4:
            out[:, 0] = spectra[:, row : row + rows]
        else:
            out[...] = spectra[:, row : row + rows]
        row += rows


def frame_of(ref, frame):
    return ref[:, frame * L : (frame + 1) * L]


def heads_kernel(v_ref, *refs):
    head_refs, held, sems = refs[:-2], refs[-2], refs[-1]
    into, out, start = [], [], 0
    for at, head_ref in enumerate(head_refs):
        lanes = slice(start, start + head_ref.shape[1])
        into.append(pltpu.make_async_copy(v_ref.at[:, lanes], held.at[:, lanes], sems.at[0, at]))
        out.append(pltpu.make_async_copy(held.at[:, lanes], head_ref, sems.at[1, at]))
        into[-1].start()
        start = lanes.stop
    for first, second in zip(into, out):
        first.wait()
        second.start()
    for copy in out:
        copy.wait()


def heads_of(voltages, widths):
    rows, span = voltages.shape[0], sum(widths)
    far = pl.BlockSpec(memory_space=pltpu.HBM)
    return pl.pallas_call(
        heads_kernel,
        in_specs=[far],
        out_specs=[far] * len(widths),
        out_shape=[jax.ShapeDtypeStruct((rows, width), jnp.bfloat16) for width in widths],
        scratch_shapes=[
            pltpu.VMEM((rows, span), jnp.bfloat16),
            pltpu.SemaphoreType.DMA((2, len(widths))),
        ],
        compiler_params=pltpu.CompilerParams(vmem_limit_bytes=58 * MIB),
        cost_estimate=pl.CostEstimate(flops=0, bytes_accessed=4 * rows * span, transcendentals=0),
        name="heads",
    )(voltages)


def first_kernel(v_ref, gain_ref, window_ref, table_ref, out_ref, held, gain, window, table, sems):
    copies = [
        pltpu.make_async_copy(frame_of(v_ref.at, tap), frame_of(held.at, tap), sems.at[tap])
        for tap in range(TAPS)
    ]
    copies.append(pltpu.make_async_copy(window_ref, window, sems.at[TAPS]))
    copies.append(pltpu.make_async_copy(gain_ref, gain, sems.at[TAPS + 1]))
    for copy in copies:
        copy.start()
    table_copy = pltpu.make_async_copy(table_ref, table, sems.at[TAPS + 2])
    table_copy.start()
    for copy in copies:
        copy.wait()
    filtered = filtered_frame([frame_of(held, tap) for tap in range(TAPS)], gain, window)
    table_copy.wait()
    put_spectra(filtered, table, [out_ref])


def first_frame(dests, voltages, gain, window, table):
    rows = voltages.shape[0]
    far = pl.BlockSpec(memory_space=pltpu.HBM)
    return pl.pallas_call(
        first_kernel,
        in_specs=[far] * 4,
        out_shape=jax.ShapeDtypeStruct((dests, 2 * CH // dests, rows), jnp.bfloat16),
        scratch_shapes=[
            pltpu.VMEM((rows, TAPS * L), jnp.bfloat16),
            pltpu.VMEM(gain.shape, jnp.float32),
            pltpu.VMEM(window.shape, jnp.float32),
            pltpu.VMEM(table.shape, jnp.bfloat16),
            pltpu.SemaphoreType.DMA((TAPS + 3,)),
        ],
        compiler_params=pltpu.CompilerParams(vmem_limit_bytes=58 * MIB),
        cost_estimate=pl.CostEstimate(
            flops=2 * rows * L * 2 * CH, bytes_accessed=4 * voltages.size, transcendentals=0
        ),
        name="first_frame",
    )(voltages, gain, window, table)


def frames_with(v_ref, later_refs):
    frames = [frame_of(v_ref, source) for source in range(v_ref.shape[1] // L)]
    for ref in later_refs:
        frames += [frame_of(ref, source) for source in range(ref.shape[1] // L)]
    return frames


def needed_of(frame, frame_count, later):
    needed = frame + TAPS - frame_count
    return [block for at, block in enumerate(later) if sum(b.shape[1] for b in later[:at]) < needed * L]


def to_tm_kernel(n_input, spectra_ref, *outs):
    n_time = len(outs)
    frames, rows = spectra_ref.shape[1], spectra_ref.shape[2]
    for t, out in enumerate(outs):
        row = lax.rem(lax.axis_index("tm") + t, n_time) * n_input
        for z in range(n_input):
            dest = row + lax.rem(lax.axis_index("inp") + z, n_input)
            for f in range(frames):
                out[z, f * rows : (f + 1) * rows] = spectra_ref[dest, f]


def to_tm(n_time, n_input, spectra):
    _, frames, cut, rows = spectra.shape
    return pl.pallas_call(
        functools.partial(to_tm_kernel, n_input),
        out_shape=[jax.ShapeDtypeStruct((n_input, frames * cut, rows), jnp.bfloat16)] * n_time,
        compiler_params=pltpu.CompilerParams(vmem_limit_bytes=24 * MIB),
        cost_estimate=pl.CostEstimate(flops=0, bytes_accessed=4 * spectra.size, transcendentals=0),
        name="to_tm",
    )(spectra)


def to_inp_kernel(n_time, *refs):
    blocks, outs = refs[:n_time], refs[n_time:]
    for z, out in enumerate(outs):
        for t in range(n_time):
            out[t] = blocks[t][z]


def to_inp(blocks):
    n_time = len(blocks)
    n_input, cut, rows = blocks[0].shape
    return pl.pallas_call(
        functools.partial(to_inp_kernel, n_time),
        out_shape=[jax.ShapeDtypeStruct((n_time, cut, rows), jnp.bfloat16)] * n_input,
        compiler_params=pltpu.CompilerParams(vmem_limit_bytes=24 * MIB),
        cost_estimate=pl.CostEstimate(
            flops=0, bytes_accessed=4 * n_time * blocks[0].size, transcendentals=0
        ),
        name="to_inp",
    )(*blocks)


def later_kernel(frame, n_later, n_out, v_ref, gain_ref, window_ref, table_ref, *refs):
    later_refs, out_refs = refs[:n_later], refs[-n_out:]
    pieces = frames_with(v_ref, later_refs)[frame : frame + TAPS]
    put_spectra(filtered_frame(pieces, gain_ref, window_ref), table_ref, out_refs)


def later_frame(frame, n_early, dests, cuts, voltages, later, gain, window, table, so_far):
    rows = voltages.shape[0]
    frame_count = voltages.shape[1] // L
    later = needed_of(frame, frame_count, later)
    whole = pl.BlockSpec(memory_space=pltpu.VMEM)
    operands = [voltages, gain, window, table, *later]
    specs = [whole] * len(operands)
    aliases = {}
    for at, block in enumerate(so_far):
        aliases[len(operands)] = at
        operands.append(block)
        specs.append(pl.BlockSpec(memory_space=pl.ANY))
    return pl.pallas_call(
        functools.partial(later_kernel, frame, len(later), len(cuts)),
        grid=(1,),
        in_specs=specs,
        out_specs=[
            pl.BlockSpec((dests, 1, cut, rows), lambda g: (0, frame - n_early, 0, 0))
            for cut in cuts
        ],
        out_shape=[
            jax.ShapeDtypeStruct((dests, frame_count - n_early, cut, rows), jnp.bfloat16)
            for cut in cuts
        ],
        input_output_aliases=aliases,
        compiler_params=pltpu.CompilerParams(vmem_limit_bytes=24 * MIB),
        cost_estimate=pl.CostEstimate(
            flops=2 * rows * L * 2 * CH, bytes_accessed=3 * voltages.size, transcendentals=0
        ),
        name="later_frame",
    )(*operands)


def steer_kernel(feed_ref, beam_ref, table_ref, out_ref):
    inputs = feed_ref.shape[1]
    chunks, wide = out_ref.shape[0], out_ref.shape[2] // 2
    feed = lax.rem(feed_ref[...], GRID).astype(jnp.float32)
    feed = jnp.broadcast_to(feed, (128, inputs)).T[:, :1].astype(jnp.int32)
    beam = lax.rem(beam_ref[...], GRID)
    pick_feed = lax.broadcasted_iota(jnp.int32, (inputs, GRID), 1) == feed
    pick_feed = jnp.where(pick_feed, 1.0, 0.0).astype(jnp.bfloat16)
    pick_beam = lax.broadcasted_iota(jnp.int32, (GRID, chunks * wide), 0) == beam
    pick_beam = jnp.where(pick_beam, 1.0, 0.0).astype(jnp.bfloat16)
    for part in range(2):
        rows = jnp.dot(pick_feed, table_ref[part], preferred_element_type=jnp.float32)
        found = jnp.dot(rows.astype(jnp.bfloat16), pick_beam, preferred_element_type=jnp.float32)
        found = found.astype(jnp.bfloat16)
        for c in range(chunks):
            out_ref[c, :, part * wide : (part + 1) * wide] = found[:, c * wide : (c + 1) * wide]


def steering(input_feed, beam_grid, table, chunks):
    inputs, beams = input_feed.shape[0], beam_grid.shape[0]
    cost = pl.CostEstimate(
        flops=4 * inputs * GRID * (GRID + beams), bytes_accessed=4 * inputs * beams, transcendentals=0
    )
    return pl.pallas_call(
        steer_kernel,
        out_shape=jax.ShapeDtypeStruct((chunks, inputs, 2 * beams // chunks), jnp.bfloat16),
        compiler_params=pltpu.CompilerParams(vmem_limit_bytes=32 * MIB),
        cost_estimate=cost,
        name="steering",
    )(input_feed.reshape(1, inputs), beam_grid.reshape(1, beams), table)


def products_kernel(
    n_time, n_input, frame_count, first, count, n_late, steer_ref, *rest
):
    early_ref, late_refs, rest = rest[0], rest[1 : n_late + 1], rest[n_late + 1 :]
    earlier_ref = rest[1] if first else None
    vis_ref, power_ref, arrived, ordered, held, ring, sems, ring_sems, in_sems, early, *late = rest[
        2 if first else 0 :
    ]
    step, steps = pl.program_id(0), pl.num_programs(0)
    chunk = step % SUB
    slots = ring.shape[0]

    def vis_copy(at, part):
        slot = at % slots
        return pltpu.make_async_copy(
            ring.at[slot, part], vis_ref.at[first + at, part], ring_sems.at[slot, part]
        )

    half = n_time * frame_count
    rows_per = 2 * half
    width = early.shape[2]
    inputs = n_input * width
    tile = 2 * SUB
    start = early_start(first)

    def steer_copy(c):
        return pltpu.make_async_copy(steer_ref.at[c], held.at[c], sems.at[c])

    @pl.when(step == 0)
    def _():
        rows = slice(start, start + early.shape[1])
        copies = [pltpu.make_async_copy(early_ref.at[:, rows], early, in_sems.at[0])]
        copies += [
            pltpu.make_async_copy(ref, late[z], in_sems.at[1 + z]) for z, ref in enumerate(late_refs)
        ]
        for copy in copies:
            copy.start()
        steer_copy(0).start()
        if first:
            power_ref[...] = earlier_ref[...]
        for copy in copies:
            copy.wait()

    def assemble(sub):
        at = sub * tile
        at_early = first * 2 - start + sub * tile
        for t in range(n_time):
            for z in range(n_input):
                source = lax.rem(lax.axis_index("inp") + n_input - z, n_input)
                slot = t * frame_count * tile
                piece = early[t * n_input + z, at_early : at_early + tile, :]
                arrived[z, slot : slot + tile, :] = piece
                for f in range(1, frame_count):
                    slot = (t * frame_count + f) * tile
                    if n_late == 1:
                        piece = late[0][t * n_input + z, f - 1, at : at + tile, :]
                        arrived[z, slot : slot + tile, :] = piece
                    else:
                        row = (f - 1) * 2 * count + at
                        arrived[source, slot : slot + tile, :] = late[z][t, row : row + tile, :]

    for sub in range(count // SUB):
        pl.when(step == sub * SUB)(functools.partial(assemble, sub))

    @pl.when(step % SUB == 0)
    def _():
        total = SUB * rows_per
        row = lax.broadcasted_iota(jnp.int32, (total, total), 0)
        column = lax.broadcasted_iota(jnp.int32, (total, total), 1)
        source = (row % half) * tile + (row // rows_per) * 2 + (row // half) % 2
        pick = jnp.where(column == source, 1.0, 0.0).astype(jnp.bfloat16)
        for z in range(n_input):
            sorted_rows = jnp.dot(pick, arrived[z], preferred_element_type=jnp.float32)
            ordered[:, z * width : (z + 1) * width] = sorted_rows.astype(jnp.bfloat16)

    @pl.when(step < SUB)
    def _():
        steer_copy(chunk).wait()

    @pl.when(step == 0)
    def _():
        for c in range(1, SUB):
            steer_copy(c).start()

    @pl.when(step >= slots)
    def _():
        for part in range(2):
            vis_copy(step - slots, part).wait()

    at = pl.multiple_of((step % SUB) * rows_per, rows_per)
    both = ordered[pl.ds(at, rows_per), :]
    re, im = both[:half], both[half:]
    right = both * jnp.asarray(1.0 / half, jnp.bfloat16)
    wide = steer_ref.shape[2] // 2
    turned = jnp.dot(ordered[...], held[chunk], preferred_element_type=jnp.float32)
    cos_part, sin_part = turned[:, :wide], turned[:, wide:]
    lanes = pl.ds(pl.multiple_of(chunk * wide, wide), wide)
    for c in range(SUB):
        rows_re = slice(c * rows_per, c * rows_per + half)
        rows_im = slice(c * rows_per + half, (c + 1) * rows_per)
        beam_re = cos_part[rows_re] - sin_part[rows_im]
        beam_im = sin_part[rows_re] + cos_part[rows_im]
        power = jnp.sum(beam_re * beam_re + beam_im * beam_im, axis=0, keepdims=True)
        row = (first // SUB + step // SUB) % 2 * SUB + c
        power_ref[pl.ds(row, 1), lanes] = power * (1.0 / half)

    block = min(inputs, 256)
    slot = step % slots
    for part in range(2):
        left = (both if part == 0 else jnp.concatenate([im, -re], 0)).T
        for j in range(0, inputs, block):
            lanes = slice(j, j + block)
            upper = jnp.dot(
                left[: j + block], right[:, lanes], preferred_element_type=jnp.float32
            ).astype(jnp.bfloat16)
            ring[slot, part, : j + block, lanes] = upper
            for i in range(0, j, block):
                mirror = upper[i : i + block].T
                ring[slot, part, lanes, i : i + block] = mirror if part == 0 else -mirror
        vis_copy(step, part).start()

    @pl.when(step == steps - 1)
    def _():
        for at in range(count - min(slots, count), count):
            for part in range(2):
                vis_copy(at, part).wait()


def early_start(first):
    return 2 * first // 16 * 16


def products(sizes, first, count, early, late, steer, so_far):
    n_time, n_input, frame_count, per_dev = sizes
    width = early.shape[2]
    inputs = n_input * width
    beams = steer.shape[0] * steer.shape[2] // 2
    rows = 2 * n_time * frame_count * SUB
    slots = min(3, count)
    start = early_start(first)
    stop = -(-2 * (first + count) // 16) * 16
    cost = pl.CostEstimate(
        flops=count * 2 * rows // SUB * inputs * (2 * inputs + 2 * beams),
        bytes_accessed=count * 4 * inputs * inputs + 4 * inputs * beams,
        transcendentals=0,
    )
    far = pl.BlockSpec(memory_space=pltpu.HBM)
    power_spec = pl.BlockSpec((2 * SUB, beams), lambda c: ((first + c) // (2 * SUB), 0))
    operands = [steer, early, *late]
    specs = [far] * len(operands)
    aliases = {}
    for at, block in enumerate(so_far):
        aliases[len(operands)] = at
        operands.append(block)
        specs.append(power_spec if at == 1 else far)
    return pl.pallas_call(
        functools.partial(
            products_kernel, n_time, n_input, frame_count, first, count, len(late)
        ),
        grid=(count,),
        in_specs=specs,
        out_specs=[far, power_spec],
        out_shape=[
            jax.ShapeDtypeStruct((per_dev, 2, inputs, inputs), jnp.bfloat16),
            jax.ShapeDtypeStruct((per_dev, beams), jnp.float32),
        ],
        scratch_shapes=[
            pltpu.VMEM((n_input, rows, width), jnp.bfloat16),
            pltpu.VMEM((rows, inputs), jnp.bfloat16),
            pltpu.VMEM(steer.shape, jnp.bfloat16),
            pltpu.VMEM((slots, 2, inputs, inputs), jnp.bfloat16),
            pltpu.SemaphoreType.DMA((SUB,)),
            pltpu.SemaphoreType.DMA((slots, 2)),
            pltpu.SemaphoreType.DMA((1 + len(late),)),
            pltpu.VMEM((n_time * n_input, stop - start, width), jnp.bfloat16),
        ]
        + [pltpu.VMEM(block.shape, jnp.bfloat16) for block in late],
        input_output_aliases=aliases,
        compiler_params=pltpu.CompilerParams(vmem_limit_bytes=58 * MIB),
        cost_estimate=cost,
        name="products",
    )(*operands)


def exchanged(block):
    return lax.all_to_all(block, AXES, 0, 0, tiled=True)


def onward(block, axis, distance):
    if distance == 0:
        return block
    devices = lax.axis_size(axis)
    return lax.ppermute(block, axis, [(i, (i + distance) % devices) for i in range(devices)])


def in_pieces(voltages, input_gain, input_feed, beam_grid):
    frame_count = voltages.shape[1] // L
    n_time = lax.axis_size("tm")
    n_input = lax.axis_size("inp")
    dests = n_time * n_input
    per_dev = CH // dests
    last = LAST_GROUP
    counts = (per_dev - last, last)
    back = [(i + 1, i) for i in range(n_time - 1)]

    window = jnp.asarray(window_table())
    table = jnp.asarray(dft_rows())
    gain = input_gain.reshape(1, -1)

    widths = ((TAPS - 2) * L, L)
    later = [lax.ppermute(head, "tm", back) for head in heads_of(voltages, widths)]
    early = exchanged(first_frame(dests, voltages, gain, window, table))

    steer = steering(input_feed, beam_grid, jnp.asarray(steer_grid(input_feed.shape[0])), SUB)
    parts = ()
    for frame in range(1, frame_count):
        cuts = [2 * count for count in counts]
        if frame == frame_count - 1:
            parts, steer = lax.optimization_barrier((parts, steer))
        parts = later_frame(frame, 1, dests, cuts, voltages, later, gain, window, table, parts)
    send, early = lax.optimization_barrier((parts[0], early))
    arrived = exchanged(send)
    blocks = [onward(block, "tm", t) for t, block in enumerate(to_tm(n_time, n_input, parts[1]))]
    onwards = to_inp(blocks)
    arrived, _ = lax.optimization_barrier((arrived, onwards))
    onwards = [onward(block, "inp", z) for z, block in enumerate(onwards)]
    sizes = (n_time, n_input, frame_count, per_dev)
    found = products(sizes, 0, counts[0], early, [arrived], steer, ())
    return products(sizes, counts[0], counts[1], early, onwards, steer, found)


def whole_channel(spectrum, steer):
    real_part, imag_part = spectrum[0], spectrum[1]
    input_count, frame_total = real_part.shape
    stacked = jnp.concatenate([real_part, imag_part], 1)
    rotated = jnp.concatenate([imag_part, -real_part], 1)
    both = jnp.concatenate([stacked, rotated], 0)
    found = lax.dot_general(
        both, stacked, (((1,), (1,)), ((), ())), preferred_element_type=jnp.float32
    )
    visible = (found / frame_total).reshape(2, input_count, input_count).astype(jnp.bfloat16)
    cos_part, sin_part = [
        lax.dot_general(
            spectrum, part, (((1,), (0,)), ((), ())), preferred_element_type=jnp.float32
        )
        for part in steer
    ]
    beam_re = cos_part[0] - sin_part[1]
    beam_im = sin_part[0] + cos_part[1]
    return visible, jnp.mean(beam_re**2 + beam_im**2, axis=0)


def at_once(voltages, input_gain, input_feed, beam_grid):
    rows = voltages.shape[0]
    frame_count = voltages.shape[1] // L
    n_time = lax.axis_size("tm")
    n_input = lax.axis_size("inp")
    dests = n_time * n_input
    per_dev = CH // dests
    later = lax.ppermute(
        voltages[:, : (TAPS - 1) * L], "tm", [(i + 1, i) for i in range(n_time - 1)]
    )
    joined = jnp.concatenate([voltages, later], 1)
    window = jnp.asarray(window_table())
    summed = jnp.zeros((rows, frame_count, L), jnp.float32)
    for tap in range(TAPS):
        piece = joined[:, tap * L : (tap + frame_count) * L].reshape(rows, frame_count, L)
        summed = summed + piece.astype(jnp.float32) * window[tap]
    filtered = (summed * input_gain[:, None, None]).astype(jnp.bfloat16)
    spectra = lax.dot_general(
        jnp.asarray(dft_rows()),
        filtered,
        (((1,), (2,)), ((), ())),
        preferred_element_type=jnp.float32,
    ).astype(jnp.bfloat16)
    blocks = exchanged(spectra.reshape(dests, per_dev * 2, rows, frame_count))
    blocks = blocks.reshape(n_time, n_input, per_dev, 2, rows, frame_count)
    owned = blocks.transpose(2, 3, 1, 4, 0, 5)
    owned = owned.reshape(per_dev, 2, n_input * rows, n_time * frame_count)
    steer = steering(input_feed, beam_grid, jnp.asarray(steer_grid(input_feed.shape[0])), 1)[0]
    steer = jnp.split(steer, 2, axis=1)
    return lax.map(lambda spectrum: whole_channel(spectrum, steer), owned)


def on_device(voltages, input_gain, input_feed, beam_grid):
    per_dev = CH // (lax.axis_size("tm") * lax.axis_size("inp"))
    slots = lax.axis_size("tm") * (voltages.shape[1] // L)
    whole_tiles = per_dev % (4 * SUB) == 0 and voltages.shape[1] >= TAPS * L and slots % 16 == 0 and beam_grid.shape[0] % (SUB * 128) == 0
    if whole_tiles and slots & (slots - 1) == 0:
        return in_pieces(voltages, input_gain, input_feed, beam_grid)
    return at_once(voltages, input_gain, input_feed, beam_grid)


def solution(mesh):
    return jax.shard_map(
        on_device,
        mesh=mesh,
        in_specs=(P("inp", "tm"), P("inp"), P(), P()),
        out_specs=(P(("tm", "inp"), None, None, None), P(("tm", "inp"), None)),
        check_vma=False,
    )
```

```python
import functools
import math

import jax
import jax.numpy as jnp
import numpy as np
from jax import lax
from jax.experimental import pallas as pl
from jax.experimental.pallas import tpu as pltpu
from jax.sharding import PartitionSpec as P

L = 1024
CH = 512
TAPS = 4
GRID = 512
SUB = 4
LAST_GROUP = 2 * SUB
AXES = ("tm", "inp")
MIB = 2**20


def window_table():
    span = TAPS * L
    pos = np.arange(span, dtype=np.float64)
    window = np.sinc((pos - span / 2) / L) * (0.5 - 0.5 * np.cos(2.0 * np.pi * pos / span))
    return window.astype(np.float32).reshape(TAPS, L)


def dft_rows():
    step = np.arange(CH)[:, None] * np.arange(L)[None, :] % L
    radians = 2.0 * np.pi * step / L
    both = np.stack([np.cos(radians), -np.sin(radians)], 1) / math.sqrt(L)
    return both.reshape(2 * CH, L).astype(jnp.bfloat16)


def steer_grid(input_count):
    step = np.arange(GRID)[:, None] * np.arange(GRID)[None, :] % GRID
    radians = 2.0 * np.pi * step / GRID
    both = np.stack([np.cos(radians), np.sin(radians)], 0) / math.sqrt(input_count)
    return both.astype(jnp.bfloat16)


def filtered_frame(pieces, gain_ref, window_ref):
    total = None
    for tap, piece in enumerate(pieces):
        term = piece.astype(jnp.float32) * window_ref[tap : tap + 1, :]
        total = term if total is None else total + term
    rows = total.shape[0]
    gain = jnp.broadcast_to(gain_ref[...], (128, rows)).T[:, :1]
    return (total * gain).astype(jnp.bfloat16)


def put_spectra(filtered, table_ref, outs):
    spectra = lax.dot_general(
        table_ref[...], filtered, (((1,), (1,)), ((), ())), preferred_element_type=jnp.float32
    ).astype(jnp.bfloat16)
    dests = outs[0].shape[0]
    spectra = spectra.reshape(dests, spectra.shape[0] // dests, spectra.shape[1])
    row = 0
    for out in outs:
        rows = out.shape[-2]
        if len(out.shape) == 4:
            out[:, 0] = spectra[:, row : row + rows]
        else:
            out[...] = spectra[:, row : row + rows]
        row += rows


def frame_of(ref, frame):
    return ref[:, frame * L : (frame + 1) * L]


def head_kernel(v_ref, head_ref, held, sems):
    pieces = sems.shape[1]
    rows = head_ref.shape[0] // pieces
    into, out = [], []
    for at in range(pieces):
        block = pl.ds(at * rows, rows)
        source = v_ref.at[block, : head_ref.shape[1]]
        into.append(pltpu.make_async_copy(source, held.at[block], sems.at[0, at]))
        out.append(pltpu.make_async_copy(held.at[block], head_ref.at[block], sems.at[1, at]))
        into[-1].start()
    for first, second in zip(into, out):
        first.wait()
        second.start()
    for copy in out:
        copy.wait()


def head_of(voltages, width):
    rows = voltages.shape[0]
    far = pl.BlockSpec(memory_space=pltpu.HBM)
    pieces = 4 if rows % 64 == 0 else 1
    return pl.pallas_call(
        head_kernel,
        in_specs=[far],
        out_specs=far,
        out_shape=jax.ShapeDtypeStruct((rows, width), jnp.bfloat16),
        scratch_shapes=[
            pltpu.VMEM((rows, width), jnp.bfloat16),
            pltpu.SemaphoreType.DMA((2, pieces)),
        ],
        compiler_params=pltpu.CompilerParams(vmem_limit_bytes=58 * MIB),
        cost_estimate=pl.CostEstimate(flops=0, bytes_accessed=4 * rows * width, transcendentals=0),
        name="head",
    )(voltages)


def first_kernel(
    v_ref, gain_ref, window_ref, table_ref, out_ref, head_ref, held, gain, window, table, sems
):
    copies = [
        pltpu.make_async_copy(frame_of(v_ref.at, tap), frame_of(held.at, tap), sems.at[tap])
        for tap in range(TAPS)
    ]
    copies.append(pltpu.make_async_copy(window_ref, window, sems.at[TAPS]))
    copies.append(pltpu.make_async_copy(gain_ref, gain, sems.at[TAPS + 1]))
    for copy in copies:
        copy.start()
    table_copy = pltpu.make_async_copy(table_ref, table, sems.at[TAPS + 2])
    table_copy.start()
    for copy in copies:
        copy.wait()
    head_copy = pltpu.make_async_copy(frame_of(held.at, TAPS - 2), head_ref, sems.at[TAPS + 3])
    head_copy.start()
    filtered = filtered_frame([frame_of(held, tap) for tap in range(TAPS)], gain, window)
    table_copy.wait()
    put_spectra(filtered, table, [out_ref])
    head_copy.wait()


def first_frame(dests, voltages, gain, window, table):
    rows = voltages.shape[0]
    far = pl.BlockSpec(memory_space=pltpu.HBM)
    return pl.pallas_call(
        first_kernel,
        in_specs=[far] * 4,
        out_specs=[pl.BlockSpec(memory_space=pltpu.VMEM), far],
        out_shape=[
            jax.ShapeDtypeStruct((dests, 2 * CH // dests, rows), jnp.bfloat16),
            jax.ShapeDtypeStruct((rows, L), jnp.bfloat16),
        ],
        scratch_shapes=[
            pltpu.VMEM((rows, TAPS * L), jnp.bfloat16),
            pltpu.VMEM(gain.shape, jnp.float32),
            pltpu.VMEM(window.shape, jnp.float32),
            pltpu.VMEM(table.shape, jnp.bfloat16),
            pltpu.SemaphoreType.DMA((TAPS + 4,)),
        ],
        compiler_params=pltpu.CompilerParams(vmem_limit_bytes=58 * MIB),
        cost_estimate=pl.CostEstimate(
            flops=2 * rows * L * 2 * CH, bytes_accessed=4 * voltages.size, transcendentals=0
        ),
        name="first_frame",
    )(voltages, gain, window, table)


def frames_with(v_ref, later_refs):
    frames = [frame_of(v_ref, source) for source in range(v_ref.shape[1] // L)]
    for ref in later_refs:
        frames += [frame_of(ref, source) for source in range(ref.shape[1] // L)]
    return frames


def needed_of(frame, frame_count, later):
    needed = frame + TAPS - frame_count
    return [block for at, block in enumerate(later) if sum(b.shape[1] for b in later[:at]) < needed * L]


def to_tm_kernel(n_input, spectra_ref, *outs):
    n_time = len(outs)
    frames, rows = spectra_ref.shape[1], spectra_ref.shape[2]
    for t, out in enumerate(outs):
        row = lax.rem(lax.axis_index("tm") + t, n_time) * n_input
        for z in range(n_input):
            dest = row + lax.rem(lax.axis_index("inp") + z, n_input)
            for f in range(frames):
                out[z, f * rows : (f + 1) * rows] = spectra_ref[dest, f]


def to_tm(n_time, n_input, spectra):
    _, frames, cut, rows = spectra.shape
    return pl.pallas_call(
        functools.partial(to_tm_kernel, n_input),
        out_shape=[jax.ShapeDtypeStruct((n_input, frames * cut, rows), jnp.bfloat16)] * n_time,
        compiler_params=pltpu.CompilerParams(vmem_limit_bytes=24 * MIB),
        cost_estimate=pl.CostEstimate(flops=0, bytes_accessed=4 * spectra.size, transcendentals=0),
        name="to_tm",
    )(spectra)


def to_inp_kernel(n_time, *refs):
    blocks, outs = refs[:n_time], refs[n_time:]
    for z, out in enumerate(outs):
        for t in range(n_time):
            out[t] = blocks[t][z]


def to_inp(blocks):
    n_time = len(blocks)
    n_input, cut, rows = blocks[0].shape
    return pl.pallas_call(
        functools.partial(to_inp_kernel, n_time),
        out_shape=[jax.ShapeDtypeStruct((n_time, cut, rows), jnp.bfloat16)] * n_input,
        compiler_params=pltpu.CompilerParams(vmem_limit_bytes=24 * MIB),
        cost_estimate=pl.CostEstimate(
            flops=0, bytes_accessed=4 * n_time * blocks[0].size, transcendentals=0
        ),
        name="to_inp",
    )(*blocks)


def later_kernel(frame, n_later, n_out, v_ref, gain_ref, window_ref, table_ref, *refs):
    later_refs, out_refs = refs[:n_later], refs[-n_out:]
    pieces = frames_with(v_ref, later_refs)[frame : frame + TAPS]
    put_spectra(filtered_frame(pieces, gain_ref, window_ref), table_ref, out_refs)


def later_frame(frame, n_early, dests, cuts, voltages, later, gain, window, table, so_far):
    rows = voltages.shape[0]
    frame_count = voltages.shape[1] // L
    later = needed_of(frame, frame_count, later)
    whole = pl.BlockSpec(memory_space=pltpu.VMEM)
    operands = [voltages, gain, window, table, *later]
    specs = [whole] * len(operands)
    aliases = {}
    for at, block in enumerate(so_far):
        aliases[len(operands)] = at
        operands.append(block)
        specs.append(pl.BlockSpec(memory_space=pl.ANY))
    return pl.pallas_call(
        functools.partial(later_kernel, frame, len(later), len(cuts)),
        grid=(1,),
        in_specs=specs,
        out_specs=[
            pl.BlockSpec((dests, 1, cut, rows), lambda g: (0, frame - n_early, 0, 0))
            for cut in cuts
        ],
        out_shape=[
            jax.ShapeDtypeStruct((dests, frame_count - n_early, cut, rows), jnp.bfloat16)
            for cut in cuts
        ],
        input_output_aliases=aliases,
        compiler_params=pltpu.CompilerParams(vmem_limit_bytes=24 * MIB),
        cost_estimate=pl.CostEstimate(
            flops=2 * rows * L * 2 * CH, bytes_accessed=3 * voltages.size, transcendentals=0
        ),
        name="later_frame",
    )(*operands)


def steer_kernel(feed_ref, beam_ref, table_ref, out_ref):
    inputs = feed_ref.shape[1]
    chunks, wide = out_ref.shape[0], out_ref.shape[2] // 2
    feed = lax.rem(feed_ref[...], GRID).astype(jnp.float32)
    feed = jnp.broadcast_to(feed, (128, inputs)).T[:, :1].astype(jnp.int32)
    beam = lax.rem(beam_ref[...], GRID)
    pick_feed = lax.broadcasted_iota(jnp.int32, (inputs, GRID), 1) == feed
    pick_feed = jnp.where(pick_feed, 1.0, 0.0).astype(jnp.bfloat16)
    pick_beam = lax.broadcasted_iota(jnp.int32, (GRID, chunks * wide), 0) == beam
    pick_beam = jnp.where(pick_beam, 1.0, 0.0).astype(jnp.bfloat16)
    for part in range(2):
        rows = jnp.dot(pick_feed, table_ref[part], preferred_element_type=jnp.float32)
        found = jnp.dot(rows.astype(jnp.bfloat16), pick_beam, preferred_element_type=jnp.float32)
        found = found.astype(jnp.bfloat16)
        for c in range(chunks):
            out_ref[c, :, part * wide : (part + 1) * wide] = found[:, c * wide : (c + 1) * wide]


def steering(input_feed, beam_grid, table, chunks):
    inputs, beams = input_feed.shape[0], beam_grid.shape[0]
    cost = pl.CostEstimate(
        flops=4 * inputs * GRID * (GRID + beams), bytes_accessed=4 * inputs * beams, transcendentals=0
    )
    return pl.pallas_call(
        steer_kernel,
        out_shape=jax.ShapeDtypeStruct((chunks, inputs, 2 * beams // chunks), jnp.bfloat16),
        compiler_params=pltpu.CompilerParams(vmem_limit_bytes=32 * MIB),
        cost_estimate=cost,
        name="steering",
    )(input_feed.reshape(1, inputs), beam_grid.reshape(1, beams), table)


def products_kernel(
    n_time, n_input, frame_count, first, count, n_late, steer_ref, *rest
):
    early_ref, late_refs, rest = rest[0], rest[1 : n_late + 1], rest[n_late + 1 :]
    shared = first % (2 * SUB) != 0
    earlier_ref = rest[1] if shared else None
    vis_ref, power_ref, arrived, ordered, held, ring, sems, ring_sems, in_sems, early, *late = rest[
        2 if first else 0 :
    ]
    step, steps = pl.program_id(0), pl.num_programs(0)
    chunk = step % SUB
    slots = ring.shape[0]

    def vis_copy(at, part):
        slot = at % slots
        return pltpu.make_async_copy(
            ring.at[slot, part], vis_ref.at[first + at, part], ring_sems.at[slot, part]
        )

    half = n_time * frame_count
    rows_per = 2 * half
    width = early.shape[2]
    inputs = n_input * width
    tile = 2 * SUB
    start = early_start(first)

    def steer_copy(c):
        return pltpu.make_async_copy(steer_ref.at[c], held.at[c], sems.at[c])

    @pl.when(step == 0)
    def _():
        rows = slice(start, start + early.shape[1])
        copies = [pltpu.make_async_copy(early_ref.at[:, rows], early, in_sems.at[0])]
        copies += [
            pltpu.make_async_copy(ref, late[z], in_sems.at[1 + z]) for z, ref in enumerate(late_refs)
        ]
        for copy in copies:
            copy.start()
        steer_copy(0).start()
        if shared:
            power_ref[...] = earlier_ref[...]
        for copy in copies:
            copy.wait()

    def assemble(sub):
        at = sub * tile
        at_early = first * 2 - start + sub * tile
        for t in range(n_time):
            for z in range(n_input):
                source = lax.rem(lax.axis_index("inp") + n_input - z, n_input)
                slot = t * frame_count * tile
                piece = early[t * n_input + z, at_early : at_early + tile, :]
                arrived[z, slot : slot + tile, :] = piece
                for f in range(1, frame_count):
                    slot = (t * frame_count + f) * tile
                    if n_late == 1:
                        piece = late[0][t * n_input + z, f - 1, at : at + tile, :]
                        arrived[z, slot : slot + tile, :] = piece
                    else:
                        row = (f - 1) * 2 * count + at
                        arrived[source, slot : slot + tile, :] = late[z][t, row : row + tile, :]

    for sub in range(count // SUB):
        pl.when(step == sub * SUB)(functools.partial(assemble, sub))

    @pl.when(step % SUB == 0)
    def _():
        total = SUB * rows_per
        row = lax.broadcasted_iota(jnp.int32, (total, total), 0)
        column = lax.broadcasted_iota(jnp.int32, (total, total), 1)
        source = (row % half) * tile + (row // rows_per) * 2 + (row // half) % 2
        pick = jnp.where(column == source, 1.0, 0.0).astype(jnp.bfloat16)
        for z in range(n_input):
            sorted_rows = jnp.dot(pick, arrived[z], preferred_element_type=jnp.float32)
            ordered[:, z * width : (z + 1) * width] = sorted_rows.astype(jnp.bfloat16)

    @pl.when(step < SUB)
    def _():
        steer_copy(chunk).wait()

    @pl.when(step == 0)
    def _():
        for c in range(1, SUB):
            steer_copy(c).start()

    @pl.when(step >= slots)
    def _():
        for part in range(2):
            vis_copy(step - slots, part).wait()

    at = pl.multiple_of((step % SUB) * rows_per, rows_per)
    both = ordered[pl.ds(at, rows_per), :]
    re, im = both[:half], both[half:]
    right = both * jnp.asarray(1.0 / half, jnp.bfloat16)
    wide = steer_ref.shape[2] // 2
    turned = jnp.dot(ordered[...], held[chunk], preferred_element_type=jnp.float32)
    cos_part, sin_part = turned[:, :wide], turned[:, wide:]
    lanes = pl.ds(pl.multiple_of(chunk * wide, wide), wide)
    for c in range(SUB):
        rows_re = slice(c * rows_per, c * rows_per + half)
        rows_im = slice(c * rows_per + half, (c + 1) * rows_per)
        beam_re = cos_part[rows_re] - sin_part[rows_im]
        beam_im = sin_part[rows_re] + cos_part[rows_im]
        power = jnp.sum(beam_re * beam_re + beam_im * beam_im, axis=0, keepdims=True)
        row = (first // SUB + step // SUB) % 2 * SUB + c
        power_ref[pl.ds(row, 1), lanes] = power * (1.0 / half)

    block = min(inputs, 256)
    slot = step % slots
    for part in range(2):
        left = (both if part == 0 else jnp.concatenate([im, -re], 0)).T
        for j in range(0, inputs, block):
            lanes = slice(j, j + block)
            upper = jnp.dot(
                left[: j + block], right[:, lanes], preferred_element_type=jnp.float32
            ).astype(jnp.bfloat16)
            ring[slot, part, : j + block, lanes] = upper
            for i in range(0, j, block):
                mirror = upper[i : i + block].T
                ring[slot, part, lanes, i : i + block] = mirror if part == 0 else -mirror
        vis_copy(step, part).start()

    @pl.when(step == steps - 1)
    def _():
        for at in range(count - min(slots, count), count):
            for part in range(2):
                vis_copy(at, part).wait()


def early_start(first):
    return 2 * first // 16 * 16


def products(sizes, first, count, early, late, steer, so_far):
    n_time, n_input, frame_count, per_dev = sizes
    width = early.shape[2]
    inputs = n_input * width
    beams = steer.shape[0] * steer.shape[2] // 2
    rows = 2 * n_time * frame_count * SUB
    slots = min(3, count)
    start = early_start(first)
    stop = -(-2 * (first + count) // 16) * 16
    cost = pl.CostEstimate(
        flops=count * 2 * rows // SUB * inputs * (2 * inputs + 2 * beams),
        bytes_accessed=count * 4 * inputs * inputs + 4 * inputs * beams,
        transcendentals=0,
    )
    far = pl.BlockSpec(memory_space=pltpu.HBM)
    any_place = pl.BlockSpec(memory_space=pl.ANY)
    power_spec = pl.BlockSpec((2 * SUB, beams), lambda c: ((first + c) // (2 * SUB), 0))
    operands = [steer, early, *late]
    specs = [far] + [any_place] * (len(operands) - 1)
    aliases = {}
    for at, block in enumerate(so_far):
        aliases[len(operands)] = at
        operands.append(block)
        specs.append(power_spec if at == 1 and first % (2 * SUB) != 0 else far)
    return pl.pallas_call(
        functools.partial(
            products_kernel, n_time, n_input, frame_count, first, count, len(late)
        ),
        grid=(count,),
        in_specs=specs,
        out_specs=[far, power_spec],
        out_shape=[
            jax.ShapeDtypeStruct((per_dev, 2, inputs, inputs), jnp.bfloat16),
            jax.ShapeDtypeStruct((per_dev, beams), jnp.float32),
        ],
        scratch_shapes=[
            pltpu.VMEM((n_input, rows, width), jnp.bfloat16),
            pltpu.VMEM((rows, inputs), jnp.bfloat16),
            pltpu.VMEM(steer.shape, jnp.bfloat16),
            pltpu.VMEM((slots, 2, inputs, inputs), jnp.bfloat16),
            pltpu.SemaphoreType.DMA((SUB,)),
            pltpu.SemaphoreType.DMA((slots, 2)),
            pltpu.SemaphoreType.DMA((1 + len(late),)),
            pltpu.VMEM((n_time * n_input, stop - start, width), jnp.bfloat16),
        ]
        + [pltpu.VMEM(block.shape, jnp.bfloat16) for block in late],
        input_output_aliases=aliases,
        compiler_params=pltpu.CompilerParams(vmem_limit_bytes=50 * MIB),
        cost_estimate=cost,
        name="products",
    )(*operands)


def exchanged(block):
    return lax.all_to_all(block, AXES, 0, 0, tiled=True)


def onward(block, axis, distance):
    if distance == 0:
        return block
    devices = lax.axis_size(axis)
    return lax.ppermute(block, axis, [(i, (i + distance) % devices) for i in range(devices)])


def in_pieces(voltages, input_gain, input_feed, beam_grid):
    frame_count = voltages.shape[1] // L
    n_time = lax.axis_size("tm")
    n_input = lax.axis_size("inp")
    dests = n_time * n_input
    per_dev = CH // dests
    last = LAST_GROUP
    counts = (per_dev - last, last)
    back = [(i + 1, i) for i in range(n_time - 1)]

    window = jnp.asarray(window_table())
    table = jnp.asarray(dft_rows())
    gain = input_gain.reshape(1, -1)

    heads = [head_of(voltages, (TAPS - 2) * L)]
    first, head = first_frame(dests, voltages, gain, window, table)
    later = [lax.ppermute(block, "tm", back) for block in (*heads, head)]
    early = exchanged(first)

    steer = steering(input_feed, beam_grid, jnp.asarray(steer_grid(input_feed.shape[0])), SUB)
    parts = ()
    for frame in range(1, frame_count):
        cuts = [2 * count for count in counts]
        if frame == frame_count - 1:
            parts, steer = lax.optimization_barrier((parts, steer))
        parts = later_frame(frame, 1, dests, cuts, voltages, later, gain, window, table, parts)
    send, early = lax.optimization_barrier((parts[0], early))
    arrived = exchanged(send)
    blocks = [onward(block, "tm", t) for t, block in enumerate(to_tm(n_time, n_input, parts[1]))]
    onwards = to_inp(blocks)
    arrived, _ = lax.optimization_barrier((arrived, onwards))
    onwards = [onward(block, "inp", z) for z, block in enumerate(onwards)]
    sizes = (n_time, n_input, frame_count, per_dev)
    found = products(sizes, 0, counts[0], early, [arrived], steer, ())
    return products(sizes, counts[0], counts[1], early, onwards, steer, found)


def whole_channel(spectrum, steer):
    real_part, imag_part = spectrum[0], spectrum[1]
    input_count, frame_total = real_part.shape
    stacked = jnp.concatenate([real_part, imag_part], 1)
    rotated = jnp.concatenate([imag_part, -real_part], 1)
    both = jnp.concatenate([stacked, rotated], 0)
    found = lax.dot_general(
        both, stacked, (((1,), (1,)), ((), ())), preferred_element_type=jnp.float32
    )
    visible = (found / frame_total).reshape(2, input_count, input_count).astype(jnp.bfloat16)
    cos_part, sin_part = [
        lax.dot_general(
            spectrum, part, (((1,), (0,)), ((), ())), preferred_element_type=jnp.float32
        )
        for part in steer
    ]
    beam_re = cos_part[0] - sin_part[1]
    beam_im = sin_part[0] + cos_part[1]
    return visible, jnp.mean(beam_re**2 + beam_im**2, axis=0)


def at_once(voltages, input_gain, input_feed, beam_grid):
    rows = voltages.shape[0]
    frame_count = voltages.shape[1] // L
    n_time = lax.axis_size("tm")
    n_input = lax.axis_size("inp")
    dests = n_time * n_input
    per_dev = CH // dests
    later = lax.ppermute(
        voltages[:, : (TAPS - 1) * L], "tm", [(i + 1, i) for i in range(n_time - 1)]
    )
    joined = jnp.concatenate([voltages, later], 1)
    window = jnp.asarray(window_table())
    summed = jnp.zeros((rows, frame_count, L), jnp.float32)
    for tap in range(TAPS):
        piece = joined[:, tap * L : (tap + frame_count) * L].reshape(rows, frame_count, L)
        summed = summed + piece.astype(jnp.float32) * window[tap]
    filtered = (summed * input_gain[:, None, None]).astype(jnp.bfloat16)
    spectra = lax.dot_general(
        jnp.asarray(dft_rows()),
        filtered,
        (((1,), (2,)), ((), ())),
        preferred_element_type=jnp.float32,
    ).astype(jnp.bfloat16)
    blocks = exchanged(spectra.reshape(dests, per_dev * 2, rows, frame_count))
    blocks = blocks.reshape(n_time, n_input, per_dev, 2, rows, frame_count)
    owned = blocks.transpose(2, 3, 1, 4, 0, 5)
    owned = owned.reshape(per_dev, 2, n_input * rows, n_time * frame_count)
    steer = steering(input_feed, beam_grid, jnp.asarray(steer_grid(input_feed.shape[0])), 1)[0]
    steer = jnp.split(steer, 2, axis=1)
    return lax.map(lambda spectrum: whole_channel(spectrum, steer), owned)


def on_device(voltages, input_gain, input_feed, beam_grid):
    per_dev = CH // (lax.axis_size("tm") * lax.axis_size("inp"))
    slots = lax.axis_size("tm") * (voltages.shape[1] // L)
    whole_tiles = per_dev % (4 * SUB) == 0 and voltages.shape[1] >= TAPS * L and slots % 16 == 0 and beam_grid.shape[0] % (SUB * 128) == 0
    if whole_tiles and slots & (slots - 1) == 0:
        return in_pieces(voltages, input_gain, input_feed, beam_grid)
    return at_once(voltages, input_gain, input_feed, beam_grid)


def solution(mesh):
    return jax.shard_map(
        on_device,
        mesh=mesh,
        in_specs=(P("inp", "tm"), P("inp"), P(), P()),
        out_specs=(P(("tm", "inp"), None, None, None), P(("tm", "inp"), None)),
        check_vma=False,
    )
```

```python
import functools
import math

import jax
import jax.numpy as jnp
import numpy as np
from jax import lax
from jax.experimental import pallas as pl
from jax.experimental.pallas import tpu as pltpu
from jax.sharding import PartitionSpec as P

L = 1024
CH = 512
TAPS = 4
GRID = 512
SUB = 4
LAST_GROUP = 2 * SUB
AXES = ("tm", "inp")
MIB = 2**20


def window_table():
    span = TAPS * L
    pos = np.arange(span, dtype=np.float64)
    window = np.sinc((pos - span / 2) / L) * (0.5 - 0.5 * np.cos(2.0 * np.pi * pos / span))
    return window.astype(np.float32).reshape(TAPS, L)


def dft_rows():
    step = np.arange(CH)[:, None] * np.arange(L)[None, :] % L
    radians = 2.0 * np.pi * step / L
    both = np.stack([np.cos(radians), -np.sin(radians)], 1) / math.sqrt(L)
    return both.reshape(2 * CH, L).astype(jnp.bfloat16)


def steer_grid(input_count):
    step = np.arange(GRID)[:, None] * np.arange(GRID)[None, :] % GRID
    radians = 2.0 * np.pi * step / GRID
    both = np.stack([np.cos(radians), np.sin(radians)], 0) / math.sqrt(input_count)
    return both.astype(jnp.bfloat16)


def filtered_frame(pieces, gain_ref, window_ref):
    total = None
    for tap, piece in enumerate(pieces):
        term = piece.astype(jnp.float32) * window_ref[tap : tap + 1, :]
        total = term if total is None else total + term
    rows = total.shape[0]
    gain = jnp.broadcast_to(gain_ref[...], (128, rows)).T[:, :1]
    return (total * gain).astype(jnp.bfloat16)


def put_spectra(filtered, table_ref, outs):
    spectra = lax.dot_general(
        table_ref[...], filtered, (((1,), (1,)), ((), ())), preferred_element_type=jnp.float32
    ).astype(jnp.bfloat16)
    dests = outs[0].shape[0]
    spectra = spectra.reshape(dests, spectra.shape[0] // dests, spectra.shape[1])
    row = 0
    for out in outs:
        rows = out.shape[-2]
        if len(out.shape) == 4:
            out[:, 0] = spectra[:, row : row + rows]
        else:
            out[...] = spectra[:, row : row + rows]
        row += rows


def frame_of(ref, frame):
    return ref[:, frame * L : (frame + 1) * L]


def head_kernel(v_ref, head_ref, held, sems):
    pieces = sems.shape[1]
    rows = head_ref.shape[0] // pieces
    into, out = [], []
    for at in range(pieces):
        block = pl.ds(at * rows, rows)
        source = v_ref.at[block, : head_ref.shape[1]]
        into.append(pltpu.make_async_copy(source, held.at[block], sems.at[0, at]))
        out.append(pltpu.make_async_copy(held.at[block], head_ref.at[block], sems.at[1, at]))
        into[-1].start()
    for first, second in zip(into, out):
        first.wait()
        second.start()
    for copy in out:
        copy.wait()


def head_of(voltages, width):
    rows = voltages.shape[0]
    far = pl.BlockSpec(memory_space=pltpu.HBM)
    pieces = 4 if rows % 64 == 0 else 1
    return pl.pallas_call(
        head_kernel,
        in_specs=[far],
        out_specs=far,
        out_shape=jax.ShapeDtypeStruct((rows, width), jnp.bfloat16),
        scratch_shapes=[
            pltpu.VMEM((rows, width), jnp.bfloat16),
            pltpu.SemaphoreType.DMA((2, pieces)),
        ],
        compiler_params=pltpu.CompilerParams(vmem_limit_bytes=58 * MIB),
        cost_estimate=pl.CostEstimate(flops=0, bytes_accessed=4 * rows * width, transcendentals=0),
        name="head",
    )(voltages)


def first_kernel(
    v_ref, gain_ref, window_ref, table_ref, out_ref, head_ref, held, gain, window, table, sems
):
    copies = [
        pltpu.make_async_copy(frame_of(v_ref.at, tap), frame_of(held.at, tap), sems.at[tap])
        for tap in range(TAPS)
    ]
    copies.append(pltpu.make_async_copy(window_ref, window, sems.at[TAPS]))
    copies.append(pltpu.make_async_copy(gain_ref, gain, sems.at[TAPS + 1]))
    for copy in copies:
        copy.start()
    table_copy = pltpu.make_async_copy(table_ref, table, sems.at[TAPS + 2])
    table_copy.start()
    for copy in copies:
        copy.wait()
    head_copy = pltpu.make_async_copy(frame_of(held.at, TAPS - 2), head_ref, sems.at[TAPS + 3])
    head_copy.start()
    filtered = filtered_frame([frame_of(held, tap) for tap in range(TAPS)], gain, window)
    table_copy.wait()
    put_spectra(filtered, table, [out_ref])
    head_copy.wait()


def first_frame(dests, voltages, gain, window, table):
    rows = voltages.shape[0]
    far = pl.BlockSpec(memory_space=pltpu.HBM)
    return pl.pallas_call(
        first_kernel,
        in_specs=[far] * 4,
        out_specs=[pl.BlockSpec(memory_space=pltpu.VMEM), far],
        out_shape=[
            jax.ShapeDtypeStruct((dests, 2 * CH // dests, rows), jnp.bfloat16),
            jax.ShapeDtypeStruct((rows, L), jnp.bfloat16),
        ],
        scratch_shapes=[
            pltpu.VMEM((rows, TAPS * L), jnp.bfloat16),
            pltpu.VMEM(gain.shape, jnp.float32),
            pltpu.VMEM(window.shape, jnp.float32),
            pltpu.VMEM(table.shape, jnp.bfloat16),
            pltpu.SemaphoreType.DMA((TAPS + 4,)),
        ],
        compiler_params=pltpu.CompilerParams(vmem_limit_bytes=58 * MIB),
        cost_estimate=pl.CostEstimate(
            flops=2 * rows * L * 2 * CH, bytes_accessed=4 * voltages.size, transcendentals=0
        ),
        name="first_frame",
    )(voltages, gain, window, table)


def frames_with(v_ref, later_refs):
    frames = [frame_of(v_ref, source) for source in range(v_ref.shape[1] // L)]
    for ref in later_refs:
        frames += [frame_of(ref, source) for source in range(ref.shape[1] // L)]
    return frames


def needed_of(frame, frame_count, later):
    needed = frame + TAPS - frame_count
    return [block for at, block in enumerate(later) if sum(b.shape[1] for b in later[:at]) < needed * L]


def to_tm_kernel(n_input, spectra_ref, *outs):
    n_time = len(outs)
    frames, rows = spectra_ref.shape[1], spectra_ref.shape[2]
    for t, out in enumerate(outs):
        row = lax.rem(lax.axis_index("tm") + t, n_time) * n_input
        for z in range(n_input):
            dest = row + lax.rem(lax.axis_index("inp") + z, n_input)
            for f in range(frames):
                out[z, f * rows : (f + 1) * rows] = spectra_ref[dest, f]


def to_tm(n_time, n_input, spectra):
    _, frames, cut, rows = spectra.shape
    return pl.pallas_call(
        functools.partial(to_tm_kernel, n_input),
        out_shape=[jax.ShapeDtypeStruct((n_input, frames * cut, rows), jnp.bfloat16)] * n_time,
        compiler_params=pltpu.CompilerParams(vmem_limit_bytes=24 * MIB),
        cost_estimate=pl.CostEstimate(flops=0, bytes_accessed=4 * spectra.size, transcendentals=0),
        name="to_tm",
    )(spectra)


def to_inp_kernel(n_time, *refs):
    blocks, outs = refs[:n_time], refs[n_time:]
    for z, out in enumerate(outs):
        for t in range(n_time):
            out[t] = blocks[t][z]


def to_inp(blocks):
    n_time = len(blocks)
    n_input, cut, rows = blocks[0].shape
    return pl.pallas_call(
        functools.partial(to_inp_kernel, n_time),
        out_shape=[jax.ShapeDtypeStruct((n_time, cut, rows), jnp.bfloat16)] * n_input,
        compiler_params=pltpu.CompilerParams(vmem_limit_bytes=24 * MIB),
        cost_estimate=pl.CostEstimate(
            flops=0, bytes_accessed=4 * n_time * blocks[0].size, transcendentals=0
        ),
        name="to_inp",
    )(*blocks)


def later_kernel(frame, n_later, n_out, v_ref, gain_ref, window_ref, table_ref, *refs):
    later_refs, out_refs = refs[:n_later], refs[-n_out:]
    pieces = frames_with(v_ref, later_refs)[frame : frame + TAPS]
    put_spectra(filtered_frame(pieces, gain_ref, window_ref), table_ref, out_refs)


def later_frame(frame, n_early, dests, cuts, voltages, later, gain, window, table, so_far):
    rows = voltages.shape[0]
    frame_count = voltages.shape[1] // L
    later = needed_of(frame, frame_count, later)
    whole = pl.BlockSpec(memory_space=pltpu.VMEM)
    operands = [voltages, gain, window, table, *later]
    specs = [whole] * len(operands)
    aliases = {}
    for at, block in enumerate(so_far):
        aliases[len(operands)] = at
        operands.append(block)
        specs.append(pl.BlockSpec(memory_space=pl.ANY))
    return pl.pallas_call(
        functools.partial(later_kernel, frame, len(later), len(cuts)),
        grid=(1,),
        in_specs=specs,
        out_specs=[
            pl.BlockSpec((dests, 1, cut, rows), lambda g: (0, frame - n_early, 0, 0))
            for cut in cuts
        ],
        out_shape=[
            jax.ShapeDtypeStruct((dests, frame_count - n_early, cut, rows), jnp.bfloat16)
            for cut in cuts
        ],
        input_output_aliases=aliases,
        compiler_params=pltpu.CompilerParams(vmem_limit_bytes=24 * MIB),
        cost_estimate=pl.CostEstimate(
            flops=2 * rows * L * 2 * CH, bytes_accessed=3 * voltages.size, transcendentals=0
        ),
        name="later_frame",
    )(*operands)


def steer_kernel(feed_ref, beam_ref, table_ref, out_ref):
    inputs = feed_ref.shape[1]
    chunks, wide = out_ref.shape[0], out_ref.shape[2] // 2
    feed = lax.rem(feed_ref[...], GRID).astype(jnp.float32)
    feed = jnp.broadcast_to(feed, (128, inputs)).T[:, :1].astype(jnp.int32)
    beam = lax.rem(beam_ref[...], GRID)
    pick_feed = lax.broadcasted_iota(jnp.int32, (inputs, GRID), 1) == feed
    pick_feed = jnp.where(pick_feed, 1.0, 0.0).astype(jnp.bfloat16)
    pick_beam = lax.broadcasted_iota(jnp.int32, (GRID, chunks * wide), 0) == beam
    pick_beam = jnp.where(pick_beam, 1.0, 0.0).astype(jnp.bfloat16)
    for part in range(2):
        rows = jnp.dot(pick_feed, table_ref[part], preferred_element_type=jnp.float32)
        found = jnp.dot(rows.astype(jnp.bfloat16), pick_beam, preferred_element_type=jnp.float32)
        found = found.astype(jnp.bfloat16)
        for c in range(chunks):
            out_ref[c, :, part * wide : (part + 1) * wide] = found[:, c * wide : (c + 1) * wide]


def steering(input_feed, beam_grid, table, chunks):
    inputs, beams = input_feed.shape[0], beam_grid.shape[0]
    cost = pl.CostEstimate(
        flops=4 * inputs * GRID * (GRID + beams), bytes_accessed=4 * inputs * beams, transcendentals=0
    )
    return pl.pallas_call(
        steer_kernel,
        out_shape=jax.ShapeDtypeStruct((chunks, inputs, 2 * beams // chunks), jnp.bfloat16),
        compiler_params=pltpu.CompilerParams(vmem_limit_bytes=32 * MIB),
        cost_estimate=cost,
        name="steering",
    )(input_feed.reshape(1, inputs), beam_grid.reshape(1, beams), table)


def products_kernel(
    n_time, n_input, frame_count, first, count, n_late, steer_ref, *rest
):
    early_ref, late_refs, rest = rest[0], rest[1 : n_late + 1], rest[n_late + 1 :]
    shared = first % (2 * SUB) != 0
    earlier_ref = rest[1] if shared else None
    vis_ref, power_ref, arrived, ordered, held, ring, sems, ring_sems, in_sems, early, *late = rest[
        2 if first else 0 :
    ]
    step, steps = pl.program_id(0), pl.num_programs(0)
    chunk = step % SUB
    slots = ring.shape[0]

    def vis_copy(at, part):
        slot = at % slots
        return pltpu.make_async_copy(
            ring.at[slot, part], vis_ref.at[first + at, part], ring_sems.at[slot, part]
        )

    half = n_time * frame_count
    rows_per = 2 * half
    width = early.shape[2]
    inputs = n_input * width
    tile = 2 * SUB
    start = early_start(first)

    def steer_copy(c):
        return pltpu.make_async_copy(steer_ref.at[c], held.at[c], sems.at[c])

    @pl.when(step == 0)
    def _():
        steer_copy(0).start()
        rows = slice(start, start + early.shape[1])
        copies = [pltpu.make_async_copy(early_ref.at[:, rows], early, in_sems.at[0])]
        copies += [
            pltpu.make_async_copy(ref, late[z], in_sems.at[1 + z]) for z, ref in enumerate(late_refs)
        ]
        for copy in copies:
            copy.start()
        if shared:
            power_ref[...] = earlier_ref[...]
        for copy in copies:
            copy.wait()

    def assemble(sub):
        at = sub * tile
        at_early = first * 2 - start + sub * tile
        for t in range(n_time):
            for z in range(n_input):
                source = lax.rem(lax.axis_index("inp") + n_input - z, n_input)
                slot = t * frame_count * tile
                piece = early[t * n_input + z, at_early : at_early + tile, :]
                arrived[z, slot : slot + tile, :] = piece
                for f in range(1, frame_count):
                    slot = (t * frame_count + f) * tile
                    if n_late == 1:
                        piece = late[0][t * n_input + z, f - 1, at : at + tile, :]
                        arrived[z, slot : slot + tile, :] = piece
                    else:
                        row = (f - 1) * 2 * count + at
                        arrived[source, slot : slot + tile, :] = late[z][t, row : row + tile, :]

    for sub in range(count // SUB):
        pl.when(step == sub * SUB)(functools.partial(assemble, sub))

    @pl.when(step % SUB == 0)
    def _():
        total = SUB * rows_per
        row = lax.broadcasted_iota(jnp.int32, (total, total), 0)
        column = lax.broadcasted_iota(jnp.int32, (total, total), 1)
        source = (row % half) * tile + (row // rows_per) * 2 + (row // half) % 2
        pick = jnp.where(column == source, 1.0, 0.0).astype(jnp.bfloat16)
        for z in range(n_input):
            sorted_rows = jnp.dot(pick, arrived[z], preferred_element_type=jnp.float32)
            ordered[:, z * width : (z + 1) * width] = sorted_rows.astype(jnp.bfloat16)

    @pl.when(step < SUB)
    def _():
        steer_copy(chunk).wait()

    @pl.when(step == 0)
    def _():
        for c in range(1, SUB):
            steer_copy(c).start()

    @pl.when(step >= slots)
    def _():
        for part in range(2):
            vis_copy(step - slots, part).wait()

    at = pl.multiple_of((step % SUB) * rows_per, rows_per)
    both = ordered[pl.ds(at, rows_per), :]
    re, im = both[:half], both[half:]
    right = both * jnp.asarray(1.0 / half, jnp.bfloat16)
    wide = steer_ref.shape[2] // 2
    turned = jnp.dot(ordered[...], held[chunk], preferred_element_type=jnp.float32)
    cos_part, sin_part = turned[:, :wide], turned[:, wide:]
    lanes = pl.ds(pl.multiple_of(chunk * wide, wide), wide)
    for c in range(SUB):
        rows_re = slice(c * rows_per, c * rows_per + half)
        rows_im = slice(c * rows_per + half, (c + 1) * rows_per)
        beam_re = cos_part[rows_re] - sin_part[rows_im]
        beam_im = sin_part[rows_re] + cos_part[rows_im]
        power = jnp.sum(beam_re * beam_re + beam_im * beam_im, axis=0, keepdims=True)
        row = (first // SUB + step // SUB) % 2 * SUB + c
        power_ref[pl.ds(row, 1), lanes] = power * (1.0 / half)

    block = min(inputs, 256)
    slot = step % slots
    for part in range(2):
        left = (both if part == 0 else jnp.concatenate([im, -re], 0)).T
        for j in range(0, inputs, block):
            lanes = slice(j, j + block)
            upper = jnp.dot(
                left[: j + block], right[:, lanes], preferred_element_type=jnp.float32
            ).astype(jnp.bfloat16)
            ring[slot, part, : j + block, lanes] = upper
            for i in range(0, j, block):
                mirror = upper[i : i + block].T
                ring[slot, part, lanes, i : i + block] = mirror if part == 0 else -mirror
        vis_copy(step, part).start()

    @pl.when(step == steps - 1)
    def _():
        for at in range(count - min(slots, count), count):
            for part in range(2):
                vis_copy(at, part).wait()


def early_start(first):
    return 2 * first // 16 * 16


def products(sizes, first, count, early, late, steer, so_far):
    n_time, n_input, frame_count, per_dev = sizes
    width = early.shape[2]
    inputs = n_input * width
    beams = steer.shape[0] * steer.shape[2] // 2
    rows = 2 * n_time * frame_count * SUB
    slots = min(3, count)
    start = early_start(first)
    stop = -(-2 * (first + count) // 16) * 16
    cost = pl.CostEstimate(
        flops=count * 2 * rows // SUB * inputs * (2 * inputs + 2 * beams),
        bytes_accessed=count * 4 * inputs * inputs + 4 * inputs * beams,
        transcendentals=0,
    )
    far = pl.BlockSpec(memory_space=pltpu.HBM)
    any_place = pl.BlockSpec(memory_space=pl.ANY)
    power_spec = pl.BlockSpec((2 * SUB, beams), lambda c: ((first + c) // (2 * SUB), 0))
    operands = [steer, early, *late]
    specs = [far] + [any_place] * (len(operands) - 1)
    aliases = {}
    for at, block in enumerate(so_far):
        aliases[len(operands)] = at
        operands.append(block)
        specs.append(power_spec if at == 1 and first % (2 * SUB) != 0 else far)
    return pl.pallas_call(
        functools.partial(
            products_kernel, n_time, n_input, frame_count, first, count, len(late)
        ),
        grid=(count,),
        in_specs=specs,
        out_specs=[far, power_spec],
        out_shape=[
            jax.ShapeDtypeStruct((per_dev, 2, inputs, inputs), jnp.bfloat16),
            jax.ShapeDtypeStruct((per_dev, beams), jnp.float32),
        ],
        scratch_shapes=[
            pltpu.VMEM((n_input, rows, width), jnp.bfloat16),
            pltpu.VMEM((rows, inputs), jnp.bfloat16),
            pltpu.VMEM(steer.shape, jnp.bfloat16),
            pltpu.VMEM((slots, 2, inputs, inputs), jnp.bfloat16),
            pltpu.SemaphoreType.DMA((SUB,)),
            pltpu.SemaphoreType.DMA((slots, 2)),
            pltpu.SemaphoreType.DMA((1 + len(late),)),
            pltpu.VMEM((n_time * n_input, stop - start, width), jnp.bfloat16),
        ]
        + [pltpu.VMEM(block.shape, jnp.bfloat16) for block in late],
        input_output_aliases=aliases,
        compiler_params=pltpu.CompilerParams(vmem_limit_bytes=50 * MIB),
        cost_estimate=cost,
        name="products",
    )(*operands)


def exchanged(block):
    return lax.all_to_all(block, AXES, 0, 0, tiled=True)


def onward(block, axis, distance):
    if distance == 0:
        return block
    devices = lax.axis_size(axis)
    return lax.ppermute(block, axis, [(i, (i + distance) % devices) for i in range(devices)])


def in_pieces(voltages, input_gain, input_feed, beam_grid):
    frame_count = voltages.shape[1] // L
    n_time = lax.axis_size("tm")
    n_input = lax.axis_size("inp")
    dests = n_time * n_input
    per_dev = CH // dests
    last = LAST_GROUP
    counts = (per_dev - last, last)
    back = [(i + 1, i) for i in range(n_time - 1)]

    window = jnp.asarray(window_table())
    table = jnp.asarray(dft_rows())
    gain = input_gain.reshape(1, -1)

    heads = [head_of(voltages, (TAPS - 2) * L)]
    first, head = first_frame(dests, voltages, gain, window, table)
    later = [lax.ppermute(block, "tm", back) for block in (*heads, head)]
    early = exchanged(first)

    steer = steering(input_feed, beam_grid, jnp.asarray(steer_grid(input_feed.shape[0])), SUB)
    parts = ()
    for frame in range(1, frame_count):
        cuts = [2 * count for count in counts]
        if frame == frame_count - 1:
            parts, steer = lax.optimization_barrier((parts, steer))
        parts = later_frame(frame, 1, dests, cuts, voltages, later, gain, window, table, parts)
    send, early = lax.optimization_barrier((parts[0], early))
    arrived = exchanged(send)
    blocks = [onward(block, "tm", t) for t, block in enumerate(to_tm(n_time, n_input, parts[1]))]
    onwards = to_inp(blocks)
    arrived, _ = lax.optimization_barrier((arrived, onwards))
    onwards = [onward(block, "inp", z) for z, block in enumerate(onwards)]
    sizes = (n_time, n_input, frame_count, per_dev)
    found = products(sizes, 0, counts[0], early, [arrived], steer, ())
    return products(sizes, counts[0], counts[1], early, onwards, steer, found)


def whole_channel(spectrum, steer):
    real_part, imag_part = spectrum[0], spectrum[1]
    input_count, frame_total = real_part.shape
    stacked = jnp.concatenate([real_part, imag_part], 1)
    rotated = jnp.concatenate([imag_part, -real_part], 1)
    both = jnp.concatenate([stacked, rotated], 0)
    found = lax.dot_general(
        both, stacked, (((1,), (1,)), ((), ())), preferred_element_type=jnp.float32
    )
    visible = (found / frame_total).reshape(2, input_count, input_count).astype(jnp.bfloat16)
    cos_part, sin_part = [
        lax.dot_general(
            spectrum, part, (((1,), (0,)), ((), ())), preferred_element_type=jnp.float32
        )
        for part in steer
    ]
    beam_re = cos_part[0] - sin_part[1]
    beam_im = sin_part[0] + cos_part[1]
    return visible, jnp.mean(beam_re**2 + beam_im**2, axis=0)


def at_once(voltages, input_gain, input_feed, beam_grid):
    rows = voltages.shape[0]
    frame_count = voltages.shape[1] // L
    n_time = lax.axis_size("tm")
    n_input = lax.axis_size("inp")
    dests = n_time * n_input
    per_dev = CH // dests
    later = lax.ppermute(
        voltages[:, : (TAPS - 1) * L], "tm", [(i + 1, i) for i in range(n_time - 1)]
    )
    joined = jnp.concatenate([voltages, later], 1)
    window = jnp.asarray(window_table())
    summed = jnp.zeros((rows, frame_count, L), jnp.float32)
    for tap in range(TAPS):
        piece = joined[:, tap * L : (tap + frame_count) * L].reshape(rows, frame_count, L)
        summed = summed + piece.astype(jnp.float32) * window[tap]
    filtered = (summed * input_gain[:, None, None]).astype(jnp.bfloat16)
    spectra = lax.dot_general(
        jnp.asarray(dft_rows()),
        filtered,
        (((1,), (2,)), ((), ())),
        preferred_element_type=jnp.float32,
    ).astype(jnp.bfloat16)
    blocks = exchanged(spectra.reshape(dests, per_dev * 2, rows, frame_count))
    blocks = blocks.reshape(n_time, n_input, per_dev, 2, rows, frame_count)
    owned = blocks.transpose(2, 3, 1, 4, 0, 5)
    owned = owned.reshape(per_dev, 2, n_input * rows, n_time * frame_count)
    steer = steering(input_feed, beam_grid, jnp.asarray(steer_grid(input_feed.shape[0])), 1)[0]
    steer = jnp.split(steer, 2, axis=1)
    return lax.map(lambda spectrum: whole_channel(spectrum, steer), owned)


def on_device(voltages, input_gain, input_feed, beam_grid):
    per_dev = CH // (lax.axis_size("tm") * lax.axis_size("inp"))
    slots = lax.axis_size("tm") * (voltages.shape[1] // L)
    whole_tiles = per_dev % (4 * SUB) == 0 and voltages.shape[1] >= TAPS * L and slots % 16 == 0 and beam_grid.shape[0] % (SUB * 128) == 0
    if whole_tiles and slots & (slots - 1) == 0:
        return in_pieces(voltages, input_gain, input_feed, beam_grid)
    return at_once(voltages, input_gain, input_feed, beam_grid)


def solution(mesh):
    return jax.shard_map(
        on_device,
        mesh=mesh,
        in_specs=(P("inp", "tm"), P("inp"), P(), P()),
        out_specs=(P(("tm", "inp"), None, None, None), P(("tm", "inp"), None)),
        check_vma=False,
    )
```
